32 devices in a mesh: dom: 8 (over z, x), bucket: 2 (over core), depth: 2 (over y).
Axes of the slice: x: 2, y: 2, z: 4, core: 2. Of those that a mesh axis runs over, the one named last changes fastest.
Arguments:
- entities: float32 [16384, 400], P(('dom', 'bucket')), may hold values from -7 to 7
- entity_state: float32 [16384], P(('dom', 'bucket')), may hold values from 0.05 to 0.5
- relations: float32 [256, 400], replicated, may hold values from 0.5 to 2
- relation_state: float32 [256], replicated, may hold values from 0.05 to 0.5
- edge_ends: int32 [2, 16384], P(None, ('dom', 'bucket')), may hold values from 0 to 1023
- relation_ids: int32 [16384], P(('dom', 'bucket')), may hold values from 0 to 255
- neg_ids: int32 [32, 1024], P(('dom', 'bucket'), 'depth'), may hold values from 0 to 1023
- edge_count: int32 [16], P(('dom', 'bucket')), may hold values from 16 to 1024, as said below
Outputs:
- new_entities: float32 [16384, 400], P(('dom', 'bucket'))
- new_state: float32 [16384], P(('dom', 'bucket'))
- new_relations: float32 [256, 400], replicated
The draws below stay inside these ranges and needn't reach their ends.
Inputs may be any that keep to these rules, and one draw needn't show every extreme that they name: `edge_count`: the live slots of a partition are its first ones; partition 0 is full in every draw.
All inputs are finite; a program needn't handle non-finite values.
Results may differ from the reference program's by a relative error of at most 0.0006.
The reference program's roundings to bfloat16 on the way count: a program that leaves them out, or rounds other values in their place, can miss the bound.
Values may be sent and summed in bfloat16 or wider, within the bound.
A program may use at most 64 MiB of HBM per device.

```python
import math
import jax
import jax.numpy as jnp
import numpy as np
from jax import lax

D = 400
NREL = 256
ENT_DEV = 1024
BLOCK = 512
BLOCKS = 2
NEG = 1024
PARTS_SIZE = 16
EDGE_DEV = 1024
ENT = 16384
EDGES = 16384
N_DOM = 8
N_BUCKET = 2


def draw_entities(key, part):
    key_row, key_value, key_dir, key_level = jax.random.split(jax.random.fold_in(key, 11), 4)
    row_scale = jnp.exp(jax.random.uniform(key_row, (ENT, 1), minval=math.log(0.12), maxval=math.log(1.2)))
    values = jax.random.normal(key_value, (ENT, D)) * row_scale
    signs = jnp.where(jax.random.normal(key_dir, (1, D)) >= 0.0, 1.0, -1.0)
    amplitude = jnp.sqrt(182.0 / D)
    level = jax.random.uniform(key_level, (ENT, 1), minval=0.8, maxval=1.2)
    slot_index = jnp.arange(ENT, dtype=jnp.int32) % ENT_DEV
    aligned = slot_index < ENT_DEV // 4
    values = jnp.where(aligned[:, None], signs * amplitude * level + 0.1 * values, values)
    return jnp.clip(values, -7.0, 7.0).astype(jnp.float32)


def draw_edge_count(key, part):
    key_base, key_shift = jax.random.split(jax.random.fold_in(key, 5))
    base_count = jax.random.randint(key_base, (PARTS_SIZE,), EDGE_DEV // 8, EDGE_DEV + 1)
    shift_count = jax.random.randint(key_shift, (PARTS_SIZE,), 0, 4)
    counts = jnp.right_shift(base_count, shift_count)
    counts = counts.at[0].set(EDGE_DEV)
    return counts.astype(jnp.int32)


def plant(entries, stream_key, least, high):
    longest = entries.shape.index(max(entries.shape))
    spots = []
    for shift in (0, 1):
        where = [jax.random.randint(jax.random.fold_in(stream_key, axis), (), 0, length) for axis, length in enumerate(entries.shape)]
        where[longest] = (where[longest] + shift) % entries.shape[longest]
        spots.append(tuple(where))
    return entries.at[spots[0]].set(least).at[spots[1]].set(high)


def level_of(key, shape, shards, smallest, high):
    loudness = 1.0
    for axis_at, blocks in shards:
        draws = jax.random.uniform(jax.random.fold_in(jax.random.fold_in(key, 6), axis_at), (blocks,), jnp.float32, smallest / len(shards), high / len(shards))
        loudness = loudness * jnp.repeat(jnp.exp(draws), shape[axis_at] // blocks).reshape((-1,) + (1,) * (len(shape) - 1 - axis_at))
    return loudness


def rank_bounds(number_of, skew):
    loads = [(1 << 20) // math.isqrt(grade ** skew) + 1 for grade in range(1, number_of + 1)]
    width = 1 + sum(loads) // (1 << 30)
    return np.cumsum(np.array([max(1, weight // width) for weight in loads]))


def ranked(rng, dims, amount, skew):
    table = rank_bounds(amount, skew)
    ticket = jax.random.randint(jax.random.fold_in(rng, 1), dims, 0, int(table[amount - 1]))
    grade = jnp.searchsorted(jnp.asarray(table, jnp.int32), ticket, side="right")
    return jax.random.permutation(jax.random.fold_in(rng, 2), amount)[grade].astype(jnp.int32)


def setup_inputs(seed: int = 0) -> dict:
    keys = jax.random.split(jax.random.key(seed), 9)
    entities = draw_entities(jax.random.fold_in(keys[8], 71), 0)
    entity_state = jnp.clip(jnp.exp(math.log(0.5) - 2.3025851 * jax.random.uniform(keys[1], (ENT,), jnp.float32) ** level_of(keys[1], (ENT,), ((0, 16),), -0.2, 0.2)), 0.05, 0.5)
    relations = jnp.clip(jnp.exp(jax.random.uniform(keys[2], (NREL, D), jnp.float32, math.log(0.5), math.log(2.0))), 0.5, 2.0)
    relation_state = jnp.clip(jnp.exp(jax.random.uniform(keys[3], (NREL,), jnp.float32, math.log(0.05), math.log(0.5))), 0.05, 0.5)
    edge_ends = plant(jax.random.randint(keys[4], (2, EDGES), 0, ENT_DEV), jax.random.fold_in(keys[4], 1), 0, ENT_DEV - 1).astype(jnp.int32)
    relation_ids = plant(ranked(keys[5], (EDGES,), NREL, 3), jax.random.fold_in(keys[5], 3), 0, NREL - 1).astype(jnp.int32)
    neg_ids = plant(jax.random.randint(keys[6], (PARTS_SIZE * BLOCKS, NEG), 0, ENT_DEV), jax.random.fold_in(keys[6], 1), 0, ENT_DEV - 1).astype(jnp.int32)
    edge_count = draw_edge_count(jax.random.fold_in(keys[8], 71), 0)
    return dict(entities=entities, entity_state=entity_state, relations=relations, relation_state=relation_state, edge_ends=edge_ends, relation_ids=relation_ids, neg_ids=neg_ids, edge_count=edge_count)


entity_rate = 0.1
relation_rate = 1.0

def block_grads(own_rows, far_rows, relations, left_ids, right_ids, rel_ids, active, negative_ids):
    left_rows = own_rows[left_ids]
    right_rows = far_rows[right_ids]
    scaling = relations[rel_ids]
    queries = (left_rows.astype(jnp.float32) * scaling).astype(jnp.bfloat16)
    negatives = far_rows[negative_ids]
    positive = lax.optimization_barrier(jnp.sum(queries.astype(jnp.float32) * right_rows.astype(jnp.float32), axis=1))
    scores = lax.dot_general(queries, negatives, (((1,), (1,)), ((), ())), preferred_element_type=jnp.float32)
    peak = jnp.maximum(positive, lax.optimization_barrier(jnp.max(scores, axis=1)))
    shifted = jnp.exp(scores - peak[:, None])
    denom = jnp.exp(positive - peak) + lax.optimization_barrier(jnp.sum(shifted, axis=1))
    weights = (shifted * (active / denom)[:, None]).astype(jnp.bfloat16)
    pos_coef = active * (jnp.exp(positive - peak) / denom - 1.0)
    query_grad = jnp.dot(weights, negatives, preferred_element_type=jnp.float32) + pos_coef[:, None] * right_rows.astype(jnp.float32)
    left_grad = query_grad * scaling
    rel_term = query_grad * left_rows.astype(jnp.float32)
    right_grad = pos_coef[:, None] * queries.astype(jnp.float32)
    neg_grad = lax.dot_general(weights, queries, (((0,), (0,)), ((), ())), preferred_element_type=jnp.float32)
    return (left_grad, rel_term, right_grad, neg_grad)

def partition_grads(own_rows, far_rows, relations, edge_rows, rel_row, neg_table, live_count):
    offsets = jnp.arange(BLOCK, dtype=jnp.int32)

    def block_step(totals_in, block_index):
        own_grad, far_grad, rel_grad = totals_in
        first_slot = (block_index * BLOCK).astype(jnp.int32)
        left_ids = lax.dynamic_slice_in_dim(edge_rows[0], first_slot, BLOCK)
        right_ids = lax.dynamic_slice_in_dim(edge_rows[1], first_slot, BLOCK)
        rel_ids = lax.dynamic_slice_in_dim(rel_row, first_slot, BLOCK)
        negative_ids = lax.dynamic_index_in_dim(neg_table, block_index, 0, keepdims=False)
        active = (first_slot + offsets < live_count).astype(jnp.float32)
        left_grad, rel_term, right_grad, neg_grad = block_grads(own_rows, far_rows, relations, left_ids, right_ids, rel_ids, active, negative_ids)
        own_grad = own_grad.at[left_ids].add(left_grad)
        far_grad = far_grad.at[right_ids].add(right_grad).at[negative_ids].add(neg_grad)
        rel_grad = rel_grad.at[rel_ids].add(rel_term)
        return ((own_grad, far_grad, rel_grad), None)
    zeros_rows = jnp.zeros((ENT_DEV, D), jnp.float32)
    start_totals = (zeros_rows, zeros_rows, jnp.zeros((NREL, D), jnp.float32))
    result, unused = lax.scan(block_step, start_totals, jnp.arange(BLOCKS, dtype=jnp.int32))
    return result

def reference(entities, entity_state, relations, relation_state, edge_ends, relation_ids, neg_ids, edge_count):
    part_count = N_DOM * N_BUCKET
    own_grid = entities.astype(jnp.bfloat16).reshape(N_DOM, N_BUCKET, ENT_DEV, D)
    far_all = jnp.roll(own_grid, N_DOM // 2, axis=0).reshape(part_count, ENT_DEV, D)
    own_all = own_grid.reshape(part_count, ENT_DEV, D)
    edge_table = edge_ends.reshape(2, part_count, EDGE_DEV).transpose(1, 0, 2)
    rel_table = relation_ids.reshape(part_count, EDGE_DEV)
    neg_tables = neg_ids.reshape(part_count, BLOCKS, NEG)

    def visit_part(rel_total, visit_item):
        own_rows, far_rows, edge_rows, rel_row, neg_table, live_count = visit_item
        own_grad, far_grad, rel_grad = partition_grads(own_rows, far_rows, relations, edge_rows, rel_row, neg_table, live_count)
        return (rel_total + rel_grad, (own_grad, far_grad))
    rel_total, grads = lax.scan(visit_part, jnp.zeros((NREL, D), jnp.float32), (own_all, far_all, edge_table, rel_table, neg_tables, edge_count))
    own_grads, far_grads = grads
    far_home = jnp.roll(far_grads.reshape(N_DOM, N_BUCKET, ENT_DEV, D), N_DOM // 2, axis=0).reshape(ENT, D)
    entity_grad = own_grads.reshape(ENT, D) + far_home
    new_state = entity_state + lax.optimization_barrier(jnp.mean(entity_grad * entity_grad, axis=1))
    new_entities = entities - entity_rate * entity_grad / jnp.sqrt(new_state)[:, None]
    rel_state = relation_state + lax.optimization_barrier(jnp.mean(rel_total * rel_total, axis=1))
    new_relations = relations - relation_rate * rel_total / jnp.sqrt(rel_state)[:, None]
    return (new_entities, new_state, new_relations)
```

```python
import functools

import jax
import jax.numpy as jnp
from jax import lax
from jax.experimental import pallas as pl
from jax.experimental.pallas import tpu as pltpu
from jax.sharding import PartitionSpec as P

entity_rate = 0.1
relation_rate = 1.0
MESH = pl.DeviceIdType.MESH
f32, bf16 = jnp.float32, jnp.bfloat16


def dot(a, b):
    return jnp.dot(a, b, preferred_element_type=f32)


def dot_nt(a, b):
    return lax.dot_general(a, b, (((1,), (1,)), ((), ())), preferred_element_type=f32)


def dot_tn(a, b):
    return lax.dot_general(a, b, (((0,), (0,)), ((), ())), preferred_element_type=f32)


def parts_of(value, terms):
    out = []
    for _ in range(terms):
        out.append(value.astype(bf16))
        value = value - out[-1].astype(f32)
    return out


def kernel(
    n_dom,
    block,
    tile,
    ent,
    info_in,
    state_in,
    rel,
    ent_out,
    state_out,
    rg_out,
    left_tab,
    far_tab,
    stage,
    info,
    far_grad,
    own_grad,
    fgb,
    from_mate,
    both,
    from_y,
    fin_send,
    fin,
    ssem,
    rsem,
):
    rows, width = ent.shape
    nrel = rel.shape[0]
    half_rows = rows // 2
    d, b, y = lax.axis_index("dom"), lax.axis_index("bucket"), lax.axis_index("depth")
    half = n_dom // 2
    d2 = lax.rem(d + half, n_dom)
    odd = lax.rem(b, 2)
    b2 = b + 1 - 2 * odd
    y2 = 1 - y
    home = odd == d // half
    away = odd != d // half
    partner, mate, ypeer = (d2, b, y), (d, b2, y), (d, b, y2)
    diag, diag2 = (d2, b2, y), (d2, b2, y2)
    mine = pl.ds(pl.multiple_of(y * half_rows, half_rows), half_rows)
    other = pl.ds(pl.multiple_of(y2 * half_rows, half_rows), half_rows)

    def copy(k, src, dst, device):
        return pltpu.make_async_remote_copy(
            src_ref=src,
            dst_ref=dst,
            send_sem=ssem.at[k],
            recv_sem=rsem.at[k],
            device_id=device,
            device_id_type=MESH,
        )

    barrier = pltpu.get_barrier_semaphore()
    for device in (partner, mate, ypeer, diag, diag2):
        pl.semaphore_signal(barrier, inc=1, device_id=device, device_id_type=MESH)
    pl.semaphore_wait(barrier, 5)

    c_stage = copy(0, stage, far_tab.at[mine], partner)
    c_left = copy(1, left_tab, far_tab, mate)
    c_cross = copy(2, far_tab.at[mine], far_tab.at[mine], ypeer)
    c_cross_in = copy(2, far_tab.at[other], far_tab.at[other], ypeer)
    c_mate0 = copy(3, far_tab.at[mine], left_tab.at[mine], mate)
    c_mate1 = copy(4, far_tab.at[other], left_tab.at[other], mate)
    c_info_home = copy(5, info_in, info.at[1], ypeer)
    c_info_away2 = copy(5, info_in, info.at[1], diag2)
    c_info_away = copy(6, info_in, info.at[0], diag)

    @pl.when(away)
    def _():
        stage[...] = ent[mine, :].astype(bf16)
        c_stage.start()
        c_info_away.start()
        c_info_away2.start()
        c_info_away.wait()
        c_info_away2.wait()

    @pl.when(home)
    def _():
        left_tab[...] = ent[...].astype(bf16)
        c_left.start()
        c_info_home.start()
        info[0] = info_in[...]
        c_info_home.wait()

    columns = jnp.concatenate([info[0], info[1]], axis=0).T
    lane_rows = lax.broadcasted_iota(jnp.int32, (1, rows), 1)
    at_zero = y == 0
    counts = jnp.zeros((1, rows), f32)
    for slot in range(2):
        both_blocks = columns[:, 8 * slot + 4 : 8 * slot + 5]
        ids = jnp.where(at_zero, both_blocks[:half_rows], both_blocks[half_rows:])
        counts += jnp.sum((ids == lane_rows).astype(f32), axis=0, keepdims=True)
    edge_cols = jnp.where(at_zero, columns[:block], columns[block:])

    @pl.when(home)
    def _():
        c_stage.wait_recv()
        c_cross.start()
        c_mate0.start()
        c_cross_in.wait_recv()
        c_mate1.start()

    @pl.when(away)
    def _():
        c_left.wait_recv()
        c_mate0.wait_recv()
        c_mate1.wait_recv()

    rel_terms = parts_of(rel[...], 3)
    lane_rel = lax.broadcasted_iota(jnp.int32, (1, nrel), 1)
    for t in range(block // tile):
        cols = edge_cols[t * tile : (t + 1) * tile]
        left_hot = (cols[:, 0:1] == lane_rows).astype(bf16)
        rel_hot = (cols[:, 2:3] == lane_rel).astype(bf16)
        right_hot = cols[:, 1:2] == lane_rows
        slot_at = y * block + t * tile + lax.broadcasted_iota(jnp.int32, (tile, 1), 0)
        active = (slot_at < cols[:, 3:4]).astype(f32)
        left_rows = dot(left_hot, left_tab[...])
        scaling = sum(dot(rel_hot, term) for term in rel_terms)
        queries = (left_rows * scaling).astype(bf16)
        scores = dot_nt(queries, far_tab[...])
        positive = jnp.sum(jnp.where(right_hot, scores, 0.0), axis=1, keepdims=True)
        masked = jnp.where(counts > 0.0, scores, -1e30)
        peak = jnp.maximum(positive, jnp.max(masked, axis=1, keepdims=True))
        shifted = jnp.exp(masked - peak)
        pos_exp = jnp.exp(positive - peak)
        denom = pos_exp + jnp.sum(counts * shifted, axis=1, keepdims=True)
        weights = (shifted * (active / denom)).astype(bf16).astype(f32)
        pos_coef = active * (pos_exp / denom - 1.0)
        coef = counts * weights + jnp.where(right_hot, pos_coef, 0.0)
        high, low = parts_of(coef, 2)
        query_grad = dot(high, far_tab[...]) + dot(low, far_tab[...])
        far_part = dot_tn(high, queries) + dot_tn(low, queries)
        g_high, g_low = parts_of(query_grad * scaling, 2)
        own_part = dot_tn(left_hot, g_high) + dot_tn(left_hot, g_low)
        r_high, r_low = parts_of(query_grad * left_rows, 2)
        rel_part = dot_tn(rel_hot, r_high) + dot_tn(rel_hot, r_low)
        if t == 0:
            far_grad[...] = far_part
            own_grad[...] = own_part
            rg_out[...] = rel_part
        else:
            far_grad[...] += far_part
            own_grad[...] += own_part
            rg_out[...] += rel_part

    fgb[...] = far_grad[...].astype(bf16)
    c_far = copy(7, fgb, from_mate, mate)
    c_far.start()
    c_far.wait()
    both[...] = (own_grad[...] + from_mate[...].astype(f32)).astype(bf16)

    c_home = copy(8, both, from_y, ypeer)
    c_away = copy(8, both.at[other], from_y.at[other], ypeer)
    c_away_in = copy(8, both.at[mine], from_y.at[mine], ypeer)
    c_fin = copy(9, fin_send, fin.at[mine], diag)
    c_fin_y = copy(10, fin.at[mine], fin.at[mine], ypeer)
    c_fin_y_in = copy(10, fin.at[other], fin.at[other], ypeer)

    def finish(grad):
        state = state_in[...].T[:, 0:1]
        updated = state + jnp.sum(grad * grad, axis=1, keepdims=True) * (1.0 / width)
        ent_out[...] = ent[...] - entity_rate * grad / jnp.sqrt(updated)
        state_out[...] = jnp.broadcast_to(updated, (rows, 128)).T[:8]

    @pl.when(home)
    def _():
        c_home.start()
        c_home.wait()
        finish(both[...].astype(f32) + from_y[...].astype(f32))
        c_left.wait_send()
        c_cross.wait_send()
        c_mate0.wait_send()
        c_mate1.wait_send()

    @pl.when(away)
    def _():
        c_away.start()
        c_away_in.wait_recv()
        fin_send[...] = (both[mine, :].astype(f32) + from_y[mine, :].astype(f32)).astype(bf16)
        c_fin.start()
        c_fin.wait_recv()
        c_fin_y.start()
        c_fin_y_in.wait_recv()
        finish(fin[...].astype(f32))
        c_stage.wait_send()
        c_away.wait_send()
        c_fin.wait_send()
        c_fin_y.wait_send()


def local(
    entities, entity_state, relations, relation_state, edge_ends, relation_ids, neg_ids, edge_count
):
    rows, width = entities.shape
    nrel = relations.shape[0]
    slots = edge_ends.shape[1]
    blocks = neg_ids.shape[0]
    block = slots // blocks
    info = jnp.concatenate(
        [
            edge_ends,
            relation_ids[None],
            jnp.broadcast_to(edge_count[:, None], (1, slots)),
            neg_ids.reshape(1, -1),
            jnp.zeros((3, slots), jnp.int32),
        ],
        axis=0,
    )
    state8 = jnp.broadcast_to(entity_state[None], (8, rows))
    vmem = pl.BlockSpec(memory_space=pltpu.VMEM)
    table = pltpu.VMEM((rows, width), bf16)
    half_table = pltpu.VMEM((rows // 2, width), bf16)
    total = pltpu.VMEM((rows, width), f32)
    new_entities, state_rows, rel_grad = pl.pallas_call(
        functools.partial(kernel, lax.axis_size("dom"), block, min(256, block)),
        out_shape=(
            jax.ShapeDtypeStruct((rows, width), f32),
            jax.ShapeDtypeStruct((8, rows), f32),
            jax.ShapeDtypeStruct((nrel, width), f32),
        ),
        in_specs=[vmem] * 4,
        out_specs=(vmem,) * 3,
        scratch_shapes=[
            table,
            table,
            half_table,
            pltpu.VMEM((2, 8, slots), jnp.int32),
            total,
            total,
            table,
            table,
            table,
            table,
            half_table,
            table,
            pltpu.SemaphoreType.DMA((12,)),
            pltpu.SemaphoreType.DMA((12,)),
        ],
        compiler_params=pltpu.CompilerParams(
            collective_id=0, has_side_effects=True, vmem_limit_bytes=56 * 1024 * 1024
        ),
    )(entities, info, state8, relations)
    rel_total = lax.psum(rel_grad, ("dom", "bucket", "depth"))
    rel_state = relation_state + jnp.mean(rel_total * rel_total, axis=1)
    new_relations = relations - relation_rate * rel_total / jnp.sqrt(rel_state)[:, None]
    return (new_entities, state_rows[0], new_relations)


def solution(mesh):
    return jax.shard_map(
        local,
        mesh=mesh,
        in_specs=(
            P(("dom", "bucket"), None),
            P(("dom", "bucket")),
            P(),
            P(),
            P(None, ("dom", "bucket")),
            P(("dom", "bucket")),
            P(("dom", "bucket"), "depth"),
            P(("dom", "bucket")),
        ),
        out_specs=(P(("dom", "bucket"), None), P(("dom", "bucket")), P()),
        check_vma=False,
    )
```

```python
import functools

import jax
import jax.numpy as jnp
from jax import lax
from jax.experimental import pallas as pl
from jax.experimental.pallas import tpu as pltpu
from jax.sharding import PartitionSpec as P

entity_rate = 0.1
relation_rate = 1.0
MESH = pl.DeviceIdType.MESH
f32, bf16 = jnp.float32, jnp.bfloat16


def dot(a, b):
    return jnp.dot(a, b, preferred_element_type=f32)


def dot_nt(a, b):
    return lax.dot_general(a, b, (((1,), (1,)), ((), ())), preferred_element_type=f32)


def parts_of(value, terms):
    out = []
    for _ in range(terms):
        out.append(value.astype(bf16))
        value = value - out[-1].astype(f32)
    return out


def kernel(
    n_dom,
    block,
    neg_half,
    chunks,
    update_relations,
    ent,
    info_in,
    state_in,
    rel,
    rel_state,
    ent_out,
    state_out,
    rel_out,
    left_tab,
    far_tab,
    stage,
    info,
    own_grad,
    fgb,
    from_mate,
    both,
    from_y,
    fin_send,
    fin,
    rg,
    rs0,
    r1,
    rs1,
    r2,
    rs2,
    tot,
    ssem,
    rsem,
):
    width, rows = ent.shape
    nrel = rel.shape[1]
    half_rows = rows // 2
    chunk = half_rows // chunks
    d, b, y = lax.axis_index("dom"), lax.axis_index("bucket"), lax.axis_index("depth")
    half = n_dom // 2
    d2 = lax.rem(d + half, n_dom)
    odd = lax.rem(b, 2)
    b2 = b + 1 - 2 * odd
    y2 = 1 - y
    home = odd == d // half
    away = odd != d // half
    partner, mate, ypeer = (d2, b, y), (d, b2, y), (d, b, y2)
    diag, diag2 = (d2, b2, y), (d2, b2, y2)
    used = [0]

    def lanes(side, j=None):
        if j is None:
            return pl.ds(pl.multiple_of(side * half_rows, half_rows), half_rows)
        return pl.ds(pl.multiple_of(side * half_rows + j * chunk, chunk), chunk)

    def slots(count):
        used[0] += count
        return used[0] - count

    def copy(k, src, dst, device):
        return pltpu.make_async_remote_copy(
            src_ref=src,
            dst_ref=dst,
            send_sem=ssem.at[k],
            recv_sem=rsem.at[k],
            device_id=device,
            device_id_type=MESH,
        )

    def move(k, src, dst, side, device):
        return [
            copy(k + j, src.at[:, lanes(side, j)], dst.at[:, lanes(side, j)], device)
            for j in range(chunks)
        ]

    ring = [lax.rem(d + k, n_dom) for k in range(n_dom)]
    barrier = pltpu.get_barrier_semaphore()
    greeted = [mate, ypeer, diag, diag2] + [(ring[k], b, y) for k in range(1, n_dom)]
    for device in greeted:
        pl.semaphore_signal(barrier, inc=1, device_id=device, device_id_type=MESH)
    pl.semaphore_wait(barrier, len(greeted))

    c_info_home = copy(slots(1), info_in, info.at[1], ypeer)
    c_info_away2 = copy(used[0] - 1, info_in, info.at[1], diag2)
    c_info_away = copy(slots(1), info_in, info.at[0], diag)
    c_left = copy(slots(1), left_tab, far_tab, mate)
    c_stage = move(slots(chunks), stage, far_tab, y, partner)
    k_cross = slots(chunks)
    c_cross = move(k_cross, far_tab, far_tab, y, ypeer)
    c_cross_in = move(k_cross, far_tab, far_tab, y2, ypeer)
    c_mate0 = move(slots(chunks), far_tab, left_tab, y, mate)
    c_mate1 = move(slots(chunks), far_tab, left_tab, y2, mate)

    @pl.when(away)
    def _():
        for j in range(chunks):
            stage[:, lanes(y, j)] = ent[:, lanes(y, j)].astype(bf16)
            c_stage[j].start()
        c_info_away.start()
        c_info_away2.start()
        c_info_away.wait()
        c_info_away2.wait()

    @pl.when(home)
    def _():
        left_tab[...] = ent[...].astype(bf16)
        c_left.start()
        c_info_home.start()
        info[0] = info_in[...]
        c_info_home.wait()

    row_at = lax.broadcasted_iota(jnp.int32, (rows, 1), 0)
    rel_at = lax.broadcasted_iota(jnp.int32, (nrel, 1), 0)
    neg_lanes = pl.ds(pl.multiple_of(y * neg_half, neg_half), neg_half)
    edge_lanes = pl.ds(pl.multiple_of(y * block, block), block)
    counts = jnp.zeros((rows, 1), f32)
    for slot in range(2):
        ids = info[slot, 4:5, neg_lanes]
        counts += jnp.sum((row_at == ids).astype(f32), axis=1, keepdims=True)
    left_ids = info[0, 0:1, edge_lanes]
    right_ids = info[0, 1:2, edge_lanes]
    rel_ids = info[0, 2:3, edge_lanes]
    live = info[0, 3:4, edge_lanes]
    slot_at = y * block + lax.broadcasted_iota(jnp.int32, (1, block), 1)
    active = (slot_at < live).astype(f32)
    left_hot = (row_at == left_ids).astype(bf16)
    rel_hot = (rel_at == rel_ids).astype(bf16)
    scales = dot(jnp.concatenate(parts_of(rel[...], 3), axis=0), rel_hot)
    scaling = scales[:width] + scales[width : 2 * width] + scales[2 * width :]

    @pl.when(home)
    def _():
        for j in range(chunks):
            c_stage[j].wait_recv()
            c_cross[j].start()
            c_mate0[j].start()
        for j in range(chunks):
            c_cross_in[j].wait_recv()
            c_mate1[j].start()

    @pl.when(away)
    def _():
        c_left.wait_recv()
        for j in range(chunks):
            c_mate0[j].wait_recv()
        for j in range(chunks):
            c_mate1[j].wait_recv()

    left_rows = dot(left_tab[...], left_hot)
    queries = (left_rows * scaling).astype(bf16)
    far = far_tab[...]
    scores = dot(far.T, queries)
    right_hot = row_at == right_ids
    positive = jnp.sum(jnp.where(right_hot, scores, 0.0), axis=0, keepdims=True)
    masked = jnp.where(counts > 0.0, scores, -1e30)
    peak = jnp.maximum(positive, jnp.max(masked, axis=0, keepdims=True))
    shifted = jnp.exp(masked - peak)
    pos_exp = jnp.exp(positive - peak)
    denom = pos_exp + jnp.sum(counts * shifted, axis=0, keepdims=True)
    weights = (shifted * (active / denom)).astype(bf16).astype(f32)
    pos_coef = active * (pos_exp / denom - 1.0)
    high, low = parts_of(counts * weights + jnp.where(right_hot, pos_coef, 0.0), 2)
    query_grad = dot(far, high) + dot(far, low)

    rel_part = dot_nt(jnp.concatenate(parts_of(query_grad * left_rows, 2), axis=0), rel_hot)
    rel_part = rel_part[:width] + rel_part[width:]
    deep = rg.shape[1]
    for side in range(2):
        rg[side, :width] = rel_part[:, side * (nrel // 2) : (side + 1) * (nrel // 2)]
        rg[side, width:] = jnp.zeros((deep - width, nrel // 2), f32)
    odd2 = 1 - odd
    c_r0 = copy(slots(1), rg.at[odd2], rs0, mate)
    c_r0.start()

    fgb[...] = (dot_nt(queries, high) + dot_nt(queries, low)).astype(bf16)
    k_far = slots(2)
    c_far = [
        copy(k_far + i, fgb.at[:, lanes(s)], from_mate.at[:, lanes(s)], mate)
        for i, s in enumerate((y2, y))
    ]
    c_far[0].start()
    c_far[1].start()

    c_r0.wait_recv()
    r1[...] = rg[odd] + rs0[...]
    half_deep = deep // 2
    part = half_deep // n_dom
    mine_deep = pl.ds(pl.multiple_of(y * half_deep, half_deep), half_deep)
    other_deep = pl.ds(pl.multiple_of(y2 * half_deep, half_deep), half_deep)
    c_r1 = copy(slots(1), r1.at[other_deep], rs1, ypeer)
    c_r1.start()

    own_grad[...] = dot_nt((query_grad * scaling).astype(bf16), left_hot)
    k_away = slots(chunks)
    c_away = move(k_away, both, from_y, y2, ypeer)
    c_away_in = move(k_away, both, from_y, y, ypeer)
    k_home = slots(2)
    c_home = [
        copy(k_home + i, both.at[:, lanes(s)], from_y.at[:, lanes(s)], ypeer)
        for i, s in enumerate((y2, y))
    ]
    c_home_in = [
        copy(k_home + i, both.at[:, lanes(s)], from_y.at[:, lanes(s)], ypeer)
        for i, s in enumerate((y, y2))
    ]
    c_fin = move(slots(chunks), fin_send, fin, y, diag)
    k_fin_y = slots(chunks)
    c_fin_y = move(k_fin_y, fin, fin, y, ypeer)
    c_fin_y_in = move(k_fin_y, fin, fin, y2, ypeer)

    for i, s in enumerate((y2, y)):
        c_far[i].wait_recv()
        side = lanes(s)
        both[:, side] = (own_grad[:, side] + from_mate[:, side].astype(f32)).astype(bf16)

        @pl.when(home)
        def _():
            c_home[i].start()

        if i == 0:

            @pl.when(away)
            def _():
                for c in c_away:
                    c.start()

    c_r1.wait_recv()
    r2[...] = r1[mine_deep, :] + rs1[...]

    def piece(at):
        return pl.ds(pl.multiple_of(at * part, part), part)

    def total_piece(at):
        return pl.ds(pl.multiple_of(y * half_deep + at * part, part), part)

    k_r2 = slots(n_dom)
    c_r2 = [
        copy(k_r2 + k, r2.at[piece(ring[k])], rs2.at[k], (ring[k], b, y)) for k in range(1, n_dom)
    ]
    for c in c_r2:
        c.start()

    @pl.when(away)
    def _():
        for j in range(chunks):
            c_away_in[j].wait_recv()
            at = lanes(y, j)
            fin_send[:, at] = (both[:, at].astype(f32) + from_y[:, at].astype(f32)).astype(bf16)
            c_fin[j].start()

    for c in c_r2:
        c.wait_recv()
    tot[odd, total_piece(d), :] = r2[piece(d), :] + jnp.sum(rs2[1:], axis=0)
    k_t2 = slots(n_dom)
    here = tot.at[odd, total_piece(d)]
    c_t2 = [copy(k_t2 + k, here, here, (ring[k], b, y)) for k in range(1, n_dom)]
    c_t2_in = []
    for k in range(1, n_dom):
        there = tot.at[odd, total_piece(ring[n_dom - k])]
        c_t2_in.append(copy(k_t2 + k, there, there, (ring[k], b, y)))
    for c in c_t2:
        c.start()

    def finish(at, grad):
        updated = state_in[:, at] + jnp.sum(grad * grad, axis=0, keepdims=True) * (1.0 / width)
        ent_out[:, at] = ent[:, at] - grad * (entity_rate / jnp.sqrt(updated))
        state_out[:, at] = updated

    @pl.when(home)
    def _():
        for i, s in enumerate((y, y2)):
            c_home_in[i].wait_recv()
            at = lanes(s)
            finish(at, both[:, at].astype(f32) + from_y[:, at].astype(f32))

    @pl.when(away)
    def _():
        for j in range(chunks):
            c_fin[j].wait_recv()
            c_fin_y[j].start()

    for c in c_t2_in:
        c.wait_recv()
    mine_t, other_t = tot.at[odd, mine_deep], tot.at[odd, other_deep]
    k_t1 = slots(1)
    c_t1 = copy(k_t1, mine_t, mine_t, ypeer)
    c_t1_in = copy(k_t1, other_t, other_t, ypeer)
    c_t1.start()

    @pl.when(away)
    def _():
        for j in range(chunks):
            finish(lanes(y, j), fin[:, lanes(y, j)].astype(f32))

    c_t1_in.wait_recv()
    k_t0 = slots(1)
    c_t0 = copy(k_t0, tot.at[odd], tot.at[odd], mate)
    c_t0_in = copy(k_t0, tot.at[odd2], tot.at[odd2], mate)
    c_t0.start()

    @pl.when(away)
    def _():
        for j in range(chunks):
            c_fin_y_in[j].wait_recv()
            finish(lanes(y2, j), fin[:, lanes(y2, j)].astype(f32))

    c_t0_in.wait_recv()
    for side in range(2):
        at = pl.ds(side * (nrel // 2), nrel // 2)
        grad = tot[side, :width]
        if update_relations:
            updated = rel_state[:, at] + jnp.sum(grad * grad, axis=0, keepdims=True) * (1.0 / width)
            rel_out[:, at] = rel[:, at] - grad * (relation_rate / jnp.sqrt(updated))
        else:
            rel_out[:, at] = grad

    @pl.when(home)
    def _():
        for c in [c_left] + c_cross + c_mate0 + c_mate1 + c_home:
            c.wait_send()

    @pl.when(away)
    def _():
        for c in c_stage + c_away + c_fin + c_fin_y:
            c.wait_send()

    for c in [c_r0, c_r1, c_t1, c_t0] + c_far + c_r2 + c_t2:
        c.wait_send()


def local(
    entities, entity_state, relations, relation_state, edge_ends, relation_ids, neg_ids, edge_count
):
    rows, width = entities.shape
    nrel = relations.shape[0]
    slots = edge_ends.shape[1]
    blocks, neg_half = neg_ids.shape
    n_dom, n_bucket, n_depth = (lax.axis_size(a) for a in ("dom", "bucket", "depth"))
    assert blocks == n_depth == 2 and n_dom % 2 == 0 and n_bucket % 2 == 0
    assert blocks * neg_half == slots
    update_relations = n_bucket == 2
    chunks = max(1, rows // 2 // 128)
    info = jnp.concatenate(
        [
            edge_ends,
            relation_ids[None],
            jnp.broadcast_to(edge_count[:, None], (1, slots)),
            neg_ids.reshape(1, -1),
            jnp.zeros((3, slots), jnp.int32),
        ],
        axis=0,
    )
    grain = 2 * 8 * n_dom
    deep = -(-width // grain) * grain
    vmem = pl.BlockSpec(memory_space=pltpu.VMEM)
    table = pltpu.VMEM((width, rows), bf16)
    half_rel = nrel // 2
    n_sems = 5 + 7 * chunks + 2 + 2 + 2 * n_dom + 4
    new_ent, new_state, new_rel = pl.pallas_call(
        functools.partial(kernel, n_dom, slots // blocks, neg_half, chunks, update_relations),
        out_shape=(
            jax.ShapeDtypeStruct((width, rows), f32),
            jax.ShapeDtypeStruct((1, rows), f32),
            jax.ShapeDtypeStruct((width, nrel), f32),
        ),
        in_specs=[vmem] * 5,
        out_specs=(vmem,) * 3,
        scratch_shapes=[
            table,
            table,
            table,
            pltpu.VMEM((2, 8, slots), jnp.int32),
            pltpu.VMEM((width, rows), f32),
            table,
            table,
            table,
            table,
            table,
            table,
            pltpu.VMEM((2, deep, half_rel), f32),
            pltpu.VMEM((deep, half_rel), f32),
            pltpu.VMEM((deep, half_rel), f32),
            pltpu.VMEM((deep // 2, half_rel), f32),
            pltpu.VMEM((deep // 2, half_rel), f32),
            pltpu.VMEM((n_dom, deep // 2 // n_dom, half_rel), f32),
            pltpu.VMEM((2, deep, half_rel), f32),
            pltpu.SemaphoreType.DMA((n_sems,)),
            pltpu.SemaphoreType.DMA((n_sems,)),
        ],
        compiler_params=pltpu.CompilerParams(
            collective_id=0, has_side_effects=True, vmem_limit_bytes=56 * 1024 * 1024
        ),
    )(entities.T, info, entity_state[None], relations.T, relation_state[None])
    if not update_relations:
        total = 0.5 * lax.psum(new_rel, "bucket")
        updated = relation_state + jnp.mean(total * total, axis=0)
        new_rel = relations.T - relation_rate * total / jnp.sqrt(updated)[None]
    return (new_ent.T, new_state[0], new_rel.T)


def solution(mesh):
    return jax.shard_map(
        local,
        mesh=mesh,
        in_specs=(
            P(("dom", "bucket"), None),
            P(("dom", "bucket")),
            P(),
            P(),
            P(None, ("dom", "bucket")),
            P(("dom", "bucket")),
            P(("dom", "bucket"), "depth"),
            P(("dom", "bucket")),
        ),
        out_specs=(P(("dom", "bucket"), None), P(("dom", "bucket")), P()),
        check_vma=False,
    )
```

```python
import functools

import jax
import jax.numpy as jnp
from jax import lax
from jax.experimental import pallas as pl
from jax.experimental.pallas import tpu as pltpu
from jax.sharding import PartitionSpec as P

entity_rate = 0.1
relation_rate = 1.0
MESH = pl.DeviceIdType.MESH
f32, bf16 = jnp.float32, jnp.bfloat16


def dot(a, b):
    return jnp.dot(a, b, preferred_element_type=f32)


def dot_nt(a, b):
    return lax.dot_general(a, b, (((1,), (1,)), ((), ())), preferred_element_type=f32)


def parts_of(value, terms):
    out = []
    for _ in range(terms):
        out.append(value.astype(bf16))
        value = value - out[-1].astype(f32)
    return out


def kernel(
    n_dom,
    block,
    neg_half,
    chunks,
    ent,
    ends_in,
    rel_ids_in,
    neg_in,
    count_in,
    rel,
    grad_out,
    rel_out,
    ent_v,
    info_in,
    left_tab,
    far_tab,
    stage,
    info,
    left_hot,
    high,
    low,
    fgb,
    from_mate,
    both,
    from_y,
    fin_send,
    fin,
    rg,
    rs0,
    r1,
    rs1,
    r2,
    rs2,
    r3,
    rs3,
    tot,
    ssem,
    rsem,
    lsem,
):
    width, rows = ent.shape
    nrel = rel.shape[1]
    half_rows = rows // 2
    chunk = half_rows // chunks
    d, b, y = lax.axis_index("dom"), lax.axis_index("bucket"), lax.axis_index("depth")
    half = n_dom // 2
    d2 = lax.rem(d + half, n_dom)
    odd = lax.rem(b, 2)
    b2 = b + 1 - 2 * odd
    y2 = 1 - y
    home = odd == d // half
    away = odd != d // half
    partner, mate, ypeer = (d2, b, y), (d, b2, y), (d, b, y2)
    diag, diag2 = (d2, b2, y), (d2, b2, y2)
    used = [0]

    def lanes(side, j=None):
        if j is None:
            return pl.ds(pl.multiple_of(side * half_rows, half_rows), half_rows)
        return pl.ds(pl.multiple_of(side * half_rows + j * chunk, chunk), chunk)

    def slots(count):
        used[0] += count
        return used[0] - count

    def copy(k, src, dst, device):
        return pltpu.make_async_remote_copy(
            src_ref=src,
            dst_ref=dst,
            send_sem=ssem.at[k],
            recv_sem=rsem.at[k],
            device_id=device,
            device_id_type=MESH,
        )

    def move(k, src, dst, side, device):
        return [
            copy(k + j, src.at[:, lanes(side, j)], dst.at[:, lanes(side, j)], device)
            for j in range(chunks)
        ]

    load_mine = pltpu.make_async_copy(ent.at[:, lanes(y)], ent_v.at[:, lanes(y)], lsem.at[0])
    load_other = pltpu.make_async_copy(ent.at[:, lanes(y2)], ent_v.at[:, lanes(y2)], lsem.at[1])
    load_mine.start()

    @pl.when(home)
    def _():
        load_other.start()

    info_in[0:2] = ends_in[...]
    info_in[2:3] = rel_ids_in[...]
    info_in[3:4] = jnp.broadcast_to(count_in[...], (1, info_in.shape[1]))
    for c in range(neg_in.shape[0]):
        info_in[4:5, c * neg_half : (c + 1) * neg_half] = neg_in[c : c + 1]
    info_in[5:] = jnp.zeros((info_in.shape[0] - 5, info_in.shape[1]), jnp.int32)

    x2 = d + 1 - 2 * lax.rem(d, 2)
    n_ring = n_dom // 2
    ring = [lax.rem(d + k, n_dom) for k in range(n_dom)]
    barrier = pltpu.get_barrier_semaphore()
    load_mine.wait()
    greeted = [mate, ypeer, diag, diag2] + [(ring[k], b, y) for k in range(1, n_dom)]
    for device in greeted:
        pl.semaphore_signal(barrier, inc=1, device_id=device, device_id_type=MESH)
    pl.semaphore_wait(barrier, len(greeted))

    c_info_home = copy(slots(1), info_in, info.at[1], ypeer)
    c_info_away2 = copy(used[0] - 1, info_in, info.at[1], diag2)
    c_info_away = copy(slots(1), info_in, info.at[0], diag)
    c_left = copy(slots(1), left_tab, far_tab, mate)
    c_stage = move(slots(chunks), stage, far_tab, y, partner)
    k_cross = slots(chunks)
    c_cross = move(k_cross, far_tab, far_tab, y, ypeer)
    c_cross_in = move(k_cross, far_tab, far_tab, y2, ypeer)
    c_mate0 = move(slots(chunks), far_tab, left_tab, y, mate)
    c_mate1 = move(slots(chunks), far_tab, left_tab, y2, mate)

    @pl.when(away)
    def _():
        for j in range(chunks):
            stage[:, lanes(y, j)] = ent_v[:, lanes(y, j)].astype(bf16)
            c_stage[j].start()
        c_info_away.start()
        c_info_away2.start()
        c_info_away.wait()
        c_info_away2.wait()

    @pl.when(home)
    def _():
        load_other.wait()
        left_tab[...] = ent_v[...].astype(bf16)
        c_left.start()
        c_info_home.start()
        info[0] = info_in[...]
        c_info_home.wait()

    row_at = lax.broadcasted_iota(jnp.int32, (rows, 1), 0)
    rel_at = lax.broadcasted_iota(jnp.int32, (nrel, 1), 0)
    neg_lanes = pl.ds(pl.multiple_of(y * neg_half, neg_half), neg_half)
    edge_lanes = pl.ds(pl.multiple_of(y * block, block), block)
    counts = jnp.zeros((rows, 1), f32)
    for slot in range(2):
        ids = info[slot, 4:5, neg_lanes]
        counts += jnp.sum((row_at == ids).astype(f32), axis=1, keepdims=True)
    left_ids = info[0, 0:1, edge_lanes]
    right_ids = info[0, 1:2, edge_lanes]
    rel_ids = info[0, 2:3, edge_lanes]
    live = info[0, 3:4, edge_lanes]
    slot_at = y * block + lax.broadcasted_iota(jnp.int32, (1, block), 1)
    active = (slot_at < live).astype(f32)
    left_hot[...] = (row_at == left_ids).astype(bf16)
    rel_hot = (rel_at == rel_ids).astype(bf16)
    scales = dot(jnp.concatenate(parts_of(rel[...], 3), axis=0), rel_hot)
    scaling = scales[:width] + scales[width : 2 * width] + scales[2 * width :]

    @pl.when(home)
    def _():
        for j in range(chunks):
            c_stage[j].wait_recv()
            c_cross[j].start()
            c_mate0[j].start()
        for j in range(chunks):
            c_cross_in[j].wait_recv()
            c_mate1[j].start()

    @pl.when(away)
    def _():
        c_left.wait_recv()
        for j in range(chunks):
            c_mate0[j].wait_recv()
        for j in range(chunks):
            c_mate1[j].wait_recv()

    left_rows = dot(left_tab[...], left_hot[...])
    queries = (left_rows * scaling).astype(bf16)
    far = far_tab[...]
    scores = dot(far.T, queries)
    right_hot = row_at == right_ids
    positive = jnp.sum(jnp.where(right_hot, scores, 0.0), axis=0, keepdims=True)
    masked = jnp.where(counts > 0.0, scores, -1e30)
    peak = jnp.maximum(positive, jnp.max(masked, axis=0, keepdims=True))
    shifted = jnp.exp(masked - peak)
    pos_exp = jnp.exp(positive - peak)
    denom = pos_exp + jnp.sum(counts * shifted, axis=0, keepdims=True)
    weights = (shifted * (active / denom)).astype(bf16).astype(f32)
    pos_coef = active * (pos_exp / denom - 1.0)
    high[...], low[...] = parts_of(counts * weights + jnp.where(right_hot, pos_coef, 0.0), 2)

    k_far = slots(2)
    c_far = []
    for i, s in enumerate((y2, y)):
        c_far.append(copy(k_far + i, fgb.at[:, lanes(s)], from_mate.at[:, lanes(s)], mate))
        far_part = dot_nt(queries, high[lanes(s), :]) + dot_nt(queries, low[lanes(s), :])
        fgb[:, lanes(s)] = far_part.astype(bf16)
        c_far[i].start()

    query_grad = dot(far, high[...]) + dot(far, low[...])
    own_terms = (query_grad * scaling).astype(bf16)

    k_away = slots(chunks)
    c_away = move(k_away, both, from_y, y2, ypeer)
    c_away_in = move(k_away, both, from_y, y, ypeer)
    k_home = slots(2)
    c_home, c_home_in = [], []
    for i, (s, o) in enumerate(((y2, y), (y, y2))):
        c_home.append(copy(k_home + i, both.at[:, lanes(s)], from_y.at[:, lanes(s)], ypeer))
        c_home_in.append(copy(k_home + i, both.at[:, lanes(o)], from_y.at[:, lanes(o)], ypeer))
    c_fin = move(slots(chunks), fin_send, fin, y, diag)
    k_fin_y = slots(chunks)
    c_fin_y = move(k_fin_y, fin, fin, y, ypeer)
    c_fin_y_in = move(k_fin_y, fin, fin, y2, ypeer)

    def own_half(i, s):
        own_part = dot_nt(own_terms, left_hot[lanes(s), :])
        c_far[i].wait_recv()
        both[:, lanes(s)] = (own_part + from_mate[:, lanes(s)].astype(f32)).astype(bf16)

        @pl.when(home)
        def _():
            c_home[i].start()

    own_half(0, y2)

    @pl.when(away)
    def _():
        for c in c_away:
            c.start()

    rel_part = dot_nt(jnp.concatenate(parts_of(query_grad * left_rows, 2), axis=0), rel_hot)
    rel_part = rel_part[:width] + rel_part[width:]
    deep = rg.shape[1]
    for side in range(2):
        rg[side, :width] = rel_part[:, side * (nrel // 2) : (side + 1) * (nrel // 2)]
        rg[side, width:] = jnp.zeros((deep - width, nrel // 2), f32)
    odd2 = 1 - odd
    c_r0 = copy(slots(1), rg.at[odd2], rs0, mate)
    c_r0.start()

    own_half(1, y)

    half_deep = deep // 2
    part = half_deep // n_ring
    x, xpeer, lap = lax.rem(d, 2), (x2, b, y), d // 2

    def half_piece(side):
        return pl.ds(pl.multiple_of(side * half_deep, half_deep), half_deep)

    def piece(side, at):
        return pl.ds(pl.multiple_of(side * half_deep + at * part, part), part)

    laps = [lax.rem(lap + k, n_ring) for k in range(n_ring)]
    peers = [(2 * at + x, b, y) for at in laps]

    c_r0.wait_recv()
    r1[...] = rg[odd] + rs0[...]
    c_r1 = copy(slots(1), r1.at[half_piece(1 - x)], rs1, xpeer)
    c_r1.start()
    c_r1.wait_recv()
    r2[...] = r1[half_piece(x), :] + rs1[...]
    k_r2 = slots(n_ring)
    c_r2 = [
        copy(k_r2 + k, r2.at[piece(0, laps[k])], rs2.at[k], peers[k]) for k in range(1, n_ring)
    ]
    for c in c_r2:
        c.start()

    @pl.when(away)
    def _():
        for j in range(chunks):
            c_away_in[j].wait_recv()
            at = lanes(y, j)
            fin_send[:, at] = (both[:, at].astype(f32) + from_y[:, at].astype(f32)).astype(bf16)
            c_fin[j].start()

    for c in c_r2:
        c.wait_recv()
    r3[...] = r2[piece(0, lap), :] + jnp.sum(rs2[1:], axis=0)
    c_r3 = copy(slots(1), r3, rs3, ypeer)
    c_r3.start()
    c_r3.wait_recv()
    tot[odd, piece(x, lap), :] = r3[...] + rs3[...]
    k_t2 = slots(n_ring)
    here = tot.at[odd, piece(x, lap)]
    c_t2, c_t2_in = [], []
    for k in range(1, n_ring):
        there = tot.at[odd, piece(x, laps[n_ring - k])]
        c_t2.append(copy(k_t2 + k, here, here, peers[k]))
        c_t2_in.append(copy(k_t2 + k, there, there, peers[k]))
        c_t2[-1].start()

    @pl.when(home)
    def _():
        c_home_in[0].wait_recv()
        at = lanes(y)
        grad_out[:, at] = both[:, at].astype(f32) + from_y[:, at].astype(f32)

    for c in c_t2_in:
        c.wait_recv()
    mine_t, other_t = tot.at[odd, half_piece(x)], tot.at[odd, half_piece(1 - x)]
    k_t1 = slots(1)
    c_t1 = copy(k_t1, mine_t, mine_t, xpeer)
    c_t1_in = copy(k_t1, other_t, other_t, xpeer)
    c_t1.start()

    @pl.when(away)
    def _():
        for j in range(chunks):
            c_fin[j].wait_recv()
            c_fin_y[j].start()

    c_t1_in.wait_recv()
    k_t0 = slots(1)
    c_t0 = copy(k_t0, tot.at[odd], tot.at[odd], mate)
    c_t0_in = copy(k_t0, tot.at[odd2], tot.at[odd2], mate)
    c_t0.start()

    @pl.when(away)
    def _():
        grad_out[:, lanes(y)] = fin[:, lanes(y)].astype(f32)
        for j in range(chunks):
            c_fin_y_in[j].wait_recv()
            grad_out[:, lanes(y2, j)] = fin[:, lanes(y2, j)].astype(f32)

    @pl.when(home)
    def _():
        c_home_in[1].wait_recv()
        at = lanes(y2)
        grad_out[:, at] = both[:, at].astype(f32) + from_y[:, at].astype(f32)

    c_t0_in.wait_recv()
    for side in range(2):
        rel_out[:, side * (nrel // 2) : (side + 1) * (nrel // 2)] = tot[side, :width]

    @pl.when(home)
    def _():
        for c in [c_left] + c_cross + c_mate0 + c_mate1 + c_home:
            c.wait_send()

    @pl.when(away)
    def _():
        for c in c_stage + c_away + c_fin + c_fin_y:
            c.wait_send()

    for c in [c_r0, c_r1, c_r3, c_t1, c_t0] + c_far + c_r2 + c_t2:
        c.wait_send()


def adagrad(rate, values, state, grad, values_out, state_out):
    updated = state[...] + jnp.sum(grad * grad, axis=0, keepdims=True) * (1.0 / grad.shape[0])
    values_out[...] = values[...] - grad * (rate / jnp.sqrt(updated))
    if state_out is not None:
        state_out[...] = updated


def update(ent, state, grad, rel, rel_state, rel_grad, ent_out, state_out, rel_out):
    adagrad(entity_rate, ent, state, grad[...], ent_out, state_out)

    @pl.when(pl.program_id(0) == 0)
    def _():
        adagrad(relation_rate, rel, rel_state, rel_grad[...], rel_out, None)


def local(
    entities, entity_state, relations, relation_state, edge_ends, relation_ids, neg_ids, edge_count
):
    rows, width = entities.shape
    nrel = relations.shape[0]
    slots = edge_ends.shape[1]
    blocks, neg_half = neg_ids.shape
    n_dom, n_bucket, n_depth = (lax.axis_size(a) for a in ("dom", "bucket", "depth"))
    assert blocks == n_depth == 2 and n_dom % 2 == 0 and n_bucket % 2 == 0
    assert blocks * neg_half == slots
    chunks = max(1, rows // 2 // 128)
    grain = 8 * n_dom
    deep = -(-width // grain) * grain
    half_rel = nrel // 2
    vmem = pl.BlockSpec(memory_space=pltpu.VMEM)
    table = pltpu.VMEM((width, rows), bf16)
    spots = pltpu.VMEM((rows, slots // blocks), bf16)
    n_sems = 16 + 7 * chunks + n_dom
    params = dict(vmem_limit_bytes=56 * 1024 * 1024)
    ent, rel = entities.T, relations.T
    grad, rel_grad = pl.pallas_call(
        functools.partial(kernel, n_dom, slots // blocks, neg_half, chunks),
        out_shape=(
            jax.ShapeDtypeStruct((width, rows), f32),
            jax.ShapeDtypeStruct((width, nrel), f32),
        ),
        in_specs=[pl.BlockSpec(memory_space=pl.ANY)] + [vmem] * 5,
        out_specs=(vmem,) * 2,
        scratch_shapes=[
            pltpu.VMEM((width, rows), f32),
            pltpu.VMEM((8, slots), jnp.int32),
            table,
            table,
            table,
            pltpu.VMEM((2, 8, slots), jnp.int32),
            spots,
            spots,
            spots,
            table,
            table,
            table,
            table,
            table,
            table,
            pltpu.VMEM((2, deep, half_rel), f32),
            pltpu.VMEM((deep, half_rel), f32),
            pltpu.VMEM((deep, half_rel), f32),
            pltpu.VMEM((deep // 2, half_rel), f32),
            pltpu.VMEM((deep // 2, half_rel), f32),
            pltpu.VMEM((n_dom // 2, deep // n_dom, half_rel), f32),
            pltpu.VMEM((deep // n_dom, half_rel), f32),
            pltpu.VMEM((deep // n_dom, half_rel), f32),
            pltpu.VMEM((2, deep, half_rel), f32),
            pltpu.SemaphoreType.DMA((n_sems,)),
            pltpu.SemaphoreType.DMA((n_sems,)),
            pltpu.SemaphoreType.DMA((2,)),
        ],
        compiler_params=pltpu.CompilerParams(collective_id=0, has_side_effects=True, **params),
    )(ent, edge_ends, relation_ids[None], neg_ids, edge_count[None], rel)
    if n_bucket != 2:
        rel_grad = 0.5 * lax.psum(rel_grad, "bucket")
    step = min(256, rows)
    wide = pl.BlockSpec((width, step), lambda i: (0, i))
    line = pl.BlockSpec((1, step), lambda i: (0, i))
    rel_all = pl.BlockSpec((width, nrel), lambda i: (0, 0))
    new_ent, new_state, new_rel = pl.pallas_call(
        update,
        grid=(rows // step,),
        out_shape=(
            jax.ShapeDtypeStruct((width, rows), f32),
            jax.ShapeDtypeStruct((1, rows), f32),
            jax.ShapeDtypeStruct((width, nrel), f32),
        ),
        in_specs=[wide, line, wide, rel_all, pl.BlockSpec((1, nrel), lambda i: (0, 0)), rel_all],
        out_specs=(wide, line, rel_all),
        compiler_params=pltpu.CompilerParams(**params),
    )(ent, entity_state[None], grad, rel, relation_state[None], rel_grad)
    return (new_ent.T, new_state[0], new_rel.T)


def solution(mesh):
    return jax.shard_map(
        local,
        mesh=mesh,
        in_specs=(
            P(("dom", "bucket"), None),
            P(("dom", "bucket")),
            P(),
            P(),
            P(None, ("dom", "bucket")),
            P(("dom", "bucket")),
            P(("dom", "bucket"), "depth"),
            P(("dom", "bucket")),
        ),
        out_specs=(P(("dom", "bucket"), None), P(("dom", "bucket")), P()),
        check_vma=False,
    )
```

```python
import functools

import jax
import jax.numpy as jnp
from jax import lax
from jax.experimental import pallas as pl
from jax.experimental.pallas import tpu as pltpu
from jax.sharding import PartitionSpec as P

entity_rate = 0.1
relation_rate = 1.0
MESH = pl.DeviceIdType.MESH
STRIP = 64
f32, bf16 = jnp.float32, jnp.bfloat16


def dot(a, b):
    return jnp.dot(a, b, preferred_element_type=f32)


def dot_nt(a, b):
    return lax.dot_general(a, b, (((1,), (1,)), ((), ())), preferred_element_type=f32)


def parts_of(value, terms):
    out = []
    for _ in range(terms):
        out.append(value.astype(bf16))
        value = value - out[-1].astype(f32)
    return out


def kernel(
    n_dom,
    block,
    neg_half,
    chunks,
    ent,
    ends_in,
    rel_ids_in,
    neg_in,
    count_in,
    rel,
    grad_out,
    rel_out,
    ent_v,
    info_in,
    left_tab,
    far_tab,
    stage,
    info,
    left_hot,
    high,
    low,
    scores,
    counts,
    fgb,
    from_mate,
    both,
    from_y,
    fin_send,
    fin,
    rg,
    rs0,
    r1,
    rs1,
    r2,
    rs2,
    r3,
    rs3,
    tot,
    ssem,
    rsem,
    lsem,
):
    width, rows = ent.shape
    nrel = rel.shape[1]
    half_rows = rows // 2
    chunk = half_rows // chunks
    d, b, y = lax.axis_index("dom"), lax.axis_index("bucket"), lax.axis_index("depth")
    half = n_dom // 2
    d2 = lax.rem(d + half, n_dom)
    odd = lax.rem(b, 2)
    b2 = b + 1 - 2 * odd
    y2 = 1 - y
    home = odd == d // half
    away = odd != d // half
    partner, mate, ypeer = (d2, b, y), (d, b2, y), (d, b, y2)
    diag, diag2 = (d2, b2, y), (d2, b2, y2)
    used = [0]

    def lanes(side, j=None):
        if j is None:
            return pl.ds(pl.multiple_of(side * half_rows, half_rows), half_rows)
        return pl.ds(pl.multiple_of(side * half_rows + j * chunk, chunk), chunk)

    def slots(count):
        used[0] += count
        return used[0] - count

    def copy(k, src, dst, device):
        return pltpu.make_async_remote_copy(
            src_ref=src,
            dst_ref=dst,
            send_sem=ssem.at[k],
            recv_sem=rsem.at[k],
            device_id=device,
            device_id_type=MESH,
        )

    def move(k, src, dst, side, device):
        return [
            copy(k + j, src.at[:, lanes(side, j)], dst.at[:, lanes(side, j)], device)
            for j in range(chunks)
        ]

    load_mine = pltpu.make_async_copy(ent.at[:, lanes(y)], ent_v.at[:, lanes(y)], lsem.at[0])
    load_other = pltpu.make_async_copy(ent.at[:, lanes(y2)], ent_v.at[:, lanes(y2)], lsem.at[1])
    load_mine.start()

    @pl.when(home)
    def _():
        load_other.start()

    info_in[0:2] = ends_in[...]
    info_in[2:3] = rel_ids_in[...]
    info_in[3:4] = jnp.broadcast_to(count_in[...], (1, info_in.shape[1]))
    for c in range(neg_in.shape[0]):
        info_in[4:5, c * neg_half : (c + 1) * neg_half] = neg_in[c : c + 1]
    info_in[5:] = jnp.zeros((info_in.shape[0] - 5, info_in.shape[1]), jnp.int32)

    x2 = d + 1 - 2 * lax.rem(d, 2)
    n_ring = n_dom // 2
    ring = [lax.rem(d + k, n_dom) for k in range(n_dom)]
    barrier = pltpu.get_barrier_semaphore()
    load_mine.wait()
    greeted = [mate, ypeer, diag, diag2] + [(ring[k], b, y) for k in range(1, n_dom)]
    for device in greeted:
        pl.semaphore_signal(barrier, inc=1, device_id=device, device_id_type=MESH)
    pl.semaphore_wait(barrier, len(greeted))

    c_info_home = copy(slots(1), info_in, info.at[1], ypeer)
    c_info_away2 = copy(used[0] - 1, info_in, info.at[1], diag2)
    c_info_away = copy(slots(1), info_in, info.at[0], diag)
    c_left = copy(slots(1), left_tab, far_tab, mate)
    c_stage = move(slots(chunks), stage, far_tab, y, partner)
    k_cross = slots(chunks)
    c_cross = move(k_cross, far_tab, far_tab, y, ypeer)
    c_cross_in = move(k_cross, far_tab, far_tab, y2, ypeer)
    c_mate0 = move(slots(chunks), far_tab, left_tab, y, mate)
    c_mate1 = move(slots(chunks), far_tab, left_tab, y2, mate)

    @pl.when(away)
    def _():
        for j in range(chunks):
            stage[:, lanes(y, j)] = ent_v[:, lanes(y, j)].astype(bf16)
            c_stage[j].start()
        c_info_away.start()
        c_info_away2.start()
        c_info_away.wait()
        c_info_away2.wait()

    @pl.when(home)
    def _():
        load_other.wait()
        left_tab[...] = ent_v[...].astype(bf16)
        c_left.start()
        c_info_home.start()
        info[0] = info_in[...]
        c_info_home.wait()

    rel_at = lax.broadcasted_iota(jnp.int32, (nrel, 1), 0)
    neg_lanes = pl.ds(pl.multiple_of(y * neg_half, neg_half), neg_half)
    edge_lanes = pl.ds(pl.multiple_of(y * block, block), block)
    left_ids = info[0, 0:1, edge_lanes]
    right_ids = info[0, 1:2, edge_lanes]
    rel_ids = info[0, 2:3, edge_lanes]
    live = info[0, 3:4, edge_lanes]
    slot_at = y * block + lax.broadcasted_iota(jnp.int32, (1, block), 1)
    active = (slot_at < live).astype(f32)
    negs = jnp.concatenate([info[slot, 4:5, neg_lanes] for slot in range(2)], axis=1)

    def strip(i):
        at = pl.ds(pl.multiple_of(i * STRIP, STRIP), STRIP)
        return at, i * STRIP + lax.broadcasted_iota(jnp.int32, (STRIP, 1), 0)

    def fold(value, join):
        return join(value.reshape(STRIP // 8, 8, block), axis=0)

    def spread(at):
        return jnp.concatenate([counts[at, :]] * (block // 128), axis=1)

    def find(i, carry):
        at, row_at = strip(i)
        hits = jnp.zeros((STRIP, 128), f32)
        for t in range(2 * neg_half // 128):
            hits += (row_at == negs[:, t * 128 : (t + 1) * 128]).astype(f32)
        counts[at, :] = jnp.broadcast_to(jnp.sum(hits, axis=1, keepdims=True), (STRIP, 128))
        left_hot[at, :] = (row_at == left_ids).astype(bf16)
        return carry

    lax.fori_loop(0, rows // STRIP, find, 0)
    rel_hot = (rel_at == rel_ids).astype(bf16)
    scales = dot(jnp.concatenate(parts_of(rel[...], 3), axis=0), rel_hot)
    scaling = scales[:width] + scales[width : 2 * width] + scales[2 * width :]

    @pl.when(home)
    def _():
        for j in range(chunks):
            c_stage[j].wait_recv()
            c_cross[j].start()
            c_mate0[j].start()
        for j in range(chunks):
            c_cross_in[j].wait_recv()
            c_mate1[j].start()

    @pl.when(away)
    def _():
        c_left.wait_recv()
        for j in range(chunks):
            c_mate0[j].wait_recv()
        for j in range(chunks):
            c_mate1[j].wait_recv()

    left_rows = dot(left_tab[...], left_hot[...])
    queries = (left_rows * scaling).astype(bf16)
    far = far_tab[...]
    scores[...] = dot(far.T, queries)

    def largest(i, carry):
        at, row_at = strip(i)
        score = scores[at, :]
        best = fold(jnp.where(spread(at) > 0.0, score, -1e30), jnp.max)
        return (
            jnp.maximum(carry[0], best),
            carry[1] + fold(jnp.where(row_at == right_ids, score, 0.0), jnp.sum),
        )

    start = (jnp.full((8, block), -1e30, f32), jnp.zeros((8, block), f32))
    best, hit = lax.fori_loop(0, rows // STRIP, largest, start)
    positive = jnp.sum(hit, axis=0, keepdims=True)
    peak = jnp.maximum(positive, jnp.max(best, axis=0, keepdims=True))

    def exponentials(i, carry):
        at, _ = strip(i)
        count = spread(at)
        shifted = jnp.exp(jnp.where(count > 0.0, scores[at, :], -1e30) - peak)
        scores[at, :] = shifted
        return carry + fold(count * shifted, jnp.sum)

    total = lax.fori_loop(0, rows // STRIP, exponentials, jnp.zeros((8, block), f32))
    pos_exp = jnp.exp(positive - peak)
    denom = pos_exp + jnp.sum(total, axis=0, keepdims=True)
    scale = active / denom
    pos_coef = active * (pos_exp / denom - 1.0)

    def coefficients(i, carry):
        at, row_at = strip(i)
        weights = (scores[at, :] * scale).astype(bf16).astype(f32)
        value = spread(at) * weights + jnp.where(row_at == right_ids, pos_coef, 0.0)
        high[at, :], low[at, :] = parts_of(value, 2)
        return carry

    lax.fori_loop(0, rows // STRIP, coefficients, 0)

    k_far = slots(2)
    c_far = []
    for i, s in enumerate((y2, y)):
        c_far.append(copy(k_far + i, fgb.at[:, lanes(s)], from_mate.at[:, lanes(s)], mate))
        far_part = dot_nt(queries, high[lanes(s), :]) + dot_nt(queries, low[lanes(s), :])
        fgb[:, lanes(s)] = far_part.astype(bf16)
        c_far[i].start()

    query_grad = dot(far, high[...]) + dot(far, low[...])
    own_terms = (query_grad * scaling).astype(bf16)

    k_away = slots(chunks)
    c_away = move(k_away, both, from_y, y2, ypeer)
    c_away_in = move(k_away, both, from_y, y, ypeer)
    k_home = slots(2)
    c_home, c_home_in = [], []
    for i, (s, o) in enumerate(((y2, y), (y, y2))):
        c_home.append(copy(k_home + i, both.at[:, lanes(s)], from_y.at[:, lanes(s)], ypeer))
        c_home_in.append(copy(k_home + i, both.at[:, lanes(o)], from_y.at[:, lanes(o)], ypeer))
    c_fin = move(slots(chunks), fin_send, fin, y, diag)
    k_fin_y = slots(chunks)
    c_fin_y = move(k_fin_y, fin, fin, y, ypeer)
    c_fin_y_in = move(k_fin_y, fin, fin, y2, ypeer)

    def own_half(i, s):
        own_part = dot_nt(own_terms, left_hot[lanes(s), :])
        c_far[i].wait_recv()
        both[:, lanes(s)] = (own_part + from_mate[:, lanes(s)].astype(f32)).astype(bf16)

        @pl.when(home)
        def _():
            c_home[i].start()

    own_half(0, y2)

    @pl.when(away)
    def _():
        for c in c_away:
            c.start()

    rel_part = dot_nt(jnp.concatenate(parts_of(query_grad * left_rows, 2), axis=0), rel_hot)
    rel_part = rel_part[:width] + rel_part[width:]
    deep = rg.shape[1]
    for side in range(2):
        rg[side, :width] = rel_part[:, side * (nrel // 2) : (side + 1) * (nrel // 2)]
        rg[side, width:] = jnp.zeros((deep - width, nrel // 2), f32)
    odd2 = 1 - odd
    c_r0 = copy(slots(1), rg.at[odd2], rs0, mate)
    c_r0.start()

    own_half(1, y)

    half_deep = deep // 2
    part = half_deep // n_ring
    x, xpeer, lap = lax.rem(d, 2), (x2, b, y), d // 2

    def half_piece(side):
        return pl.ds(pl.multiple_of(side * half_deep, half_deep), half_deep)

    def piece(side, at):
        return pl.ds(pl.multiple_of(side * half_deep + at * part, part), part)

    laps = [lax.rem(lap + k, n_ring) for k in range(n_ring)]
    peers = [(2 * at + x, b, y) for at in laps]

    c_r0.wait_recv()
    r1[...] = rg[odd] + rs0[...]
    c_r1 = copy(slots(1), r1.at[half_piece(1 - x)], rs1, xpeer)
    c_r1.start()
    c_r1.wait_recv()
    r2[...] = r1[half_piece(x), :] + rs1[...]
    k_r2 = slots(n_ring)
    c_r2 = [
        copy(k_r2 + k, r2.at[piece(0, laps[k])], rs2.at[k], peers[k]) for k in range(1, n_ring)
    ]
    for c in c_r2:
        c.start()

    @pl.when(away)
    def _():
        for j in range(chunks):
            c_away_in[j].wait_recv()
            at = lanes(y, j)
            fin_send[:, at] = (both[:, at].astype(f32) + from_y[:, at].astype(f32)).astype(bf16)
            c_fin[j].start()

    for c in c_r2:
        c.wait_recv()
    r3[...] = r2[piece(0, lap), :] + jnp.sum(rs2[1:], axis=0)
    c_r3 = copy(slots(1), r3, rs3, ypeer)
    c_r3.start()
    c_r3.wait_recv()
    tot[odd, piece(x, lap), :] = r3[...] + rs3[...]
    k_t2 = slots(n_ring)
    here = tot.at[odd, piece(x, lap)]
    c_t2, c_t2_in = [], []
    for k in range(1, n_ring):
        there = tot.at[odd, piece(x, laps[n_ring - k])]
        c_t2.append(copy(k_t2 + k, here, here, peers[k]))
        c_t2_in.append(copy(k_t2 + k, there, there, peers[k]))
        c_t2[-1].start()

    @pl.when(home)
    def _():
        c_home_in[0].wait_recv()
        at = lanes(y)
        grad_out[:, at] = (both[:, at].astype(f32) + from_y[:, at].astype(f32)).astype(bf16)

    for c in c_t2_in:
        c.wait_recv()
    mine_t, other_t = tot.at[odd, half_piece(x)], tot.at[odd, half_piece(1 - x)]
    k_t1 = slots(1)
    c_t1 = copy(k_t1, mine_t, mine_t, xpeer)
    c_t1_in = copy(k_t1, other_t, other_t, xpeer)
    c_t1.start()

    @pl.when(away)
    def _():
        for j in range(chunks):
            c_fin[j].wait_recv()
            c_fin_y[j].start()

    c_t1_in.wait_recv()
    k_t0 = slots(1)
    c_t0 = copy(k_t0, tot.at[odd], tot.at[odd], mate)
    c_t0_in = copy(k_t0, tot.at[odd2], tot.at[odd2], mate)
    c_t0.start()

    @pl.when(away)
    def _():
        grad_out[:, lanes(y)] = fin[:, lanes(y)]
        for j in range(chunks):
            c_fin_y_in[j].wait_recv()
            grad_out[:, lanes(y2, j)] = fin[:, lanes(y2, j)]

    @pl.when(home)
    def _():
        c_home_in[1].wait_recv()
        at = lanes(y2)
        grad_out[:, at] = (both[:, at].astype(f32) + from_y[:, at].astype(f32)).astype(bf16)

    c_t0_in.wait_recv()
    for side in range(2):
        rel_out[:, side * (nrel // 2) : (side + 1) * (nrel // 2)] = tot[side, :width]

    @pl.when(home)
    def _():
        for c in [c_left] + c_cross + c_mate0 + c_mate1 + c_home:
            c.wait_send()

    @pl.when(away)
    def _():
        for c in c_stage + c_away + c_fin + c_fin_y:
            c.wait_send()

    for c in [c_r0, c_r1, c_r3, c_t1, c_t0] + c_far + c_r2 + c_t2:
        c.wait_send()


def adagrad(rate, values, state, grad, values_out, state_out):
    updated = state[...] + jnp.sum(grad * grad, axis=0, keepdims=True) * (1.0 / grad.shape[0])
    values_out[...] = values[...] - grad * (rate / jnp.sqrt(updated))
    if state_out is not None:
        state_out[...] = updated


def update(ent, state, grad, rel, rel_state, rel_grad, ent_out, state_out, rel_out):
    adagrad(entity_rate, ent, state, grad[...].astype(f32), ent_out, state_out)

    @pl.when(pl.program_id(0) == 0)
    def _():
        adagrad(relation_rate, rel, rel_state, rel_grad[...], rel_out, None)


def local(
    entities, entity_state, relations, relation_state, edge_ends, relation_ids, neg_ids, edge_count
):
    rows, width = entities.shape
    nrel = relations.shape[0]
    slots = edge_ends.shape[1]
    blocks, neg_half = neg_ids.shape
    n_dom, n_bucket, n_depth = (lax.axis_size(a) for a in ("dom", "bucket", "depth"))
    assert blocks == n_depth == 2 and n_dom % 2 == 0 and n_bucket % 2 == 0
    assert blocks * neg_half == slots
    chunks = max(1, rows // 2 // 128)
    grain = 8 * n_dom
    deep = -(-width // grain) * grain
    half_rel = nrel // 2
    vmem = pl.BlockSpec(memory_space=pltpu.VMEM)
    table = pltpu.VMEM((width, rows), bf16)
    spots = pltpu.VMEM((rows, slots // blocks), bf16)
    n_sems = 16 + 7 * chunks + n_dom
    params = dict(vmem_limit_bytes=56 * 1024 * 1024)
    ent, rel = entities.T, relations.T
    grad, rel_grad = pl.pallas_call(
        functools.partial(kernel, n_dom, slots // blocks, neg_half, chunks),
        out_shape=(
            jax.ShapeDtypeStruct((width, rows), bf16),
            jax.ShapeDtypeStruct((width, nrel), f32),
        ),
        in_specs=[pl.BlockSpec(memory_space=pl.ANY)] + [vmem] * 5,
        out_specs=(vmem,) * 2,
        scratch_shapes=[
            pltpu.VMEM((width, rows), f32),
            pltpu.VMEM((8, slots), jnp.int32),
            table,
            table,
            table,
            pltpu.VMEM((2, 8, slots), jnp.int32),
            spots,
            spots,
            spots,
            pltpu.VMEM((rows, slots // blocks), f32),
            pltpu.VMEM((rows, 128), f32),
            table,
            table,
            table,
            table,
            table,
            table,
            pltpu.VMEM((2, deep, half_rel), f32),
            pltpu.VMEM((deep, half_rel), f32),
            pltpu.VMEM((deep, half_rel), f32),
            pltpu.VMEM((deep // 2, half_rel), f32),
            pltpu.VMEM((deep // 2, half_rel), f32),
            pltpu.VMEM((n_dom // 2, deep // n_dom, half_rel), f32),
            pltpu.VMEM((deep // n_dom, half_rel), f32),
            pltpu.VMEM((deep // n_dom, half_rel), f32),
            pltpu.VMEM((2, deep, half_rel), f32),
            pltpu.SemaphoreType.DMA((n_sems,)),
            pltpu.SemaphoreType.DMA((n_sems,)),
            pltpu.SemaphoreType.DMA((2,)),
        ],
        compiler_params=pltpu.CompilerParams(collective_id=0, has_side_effects=True, **params),
    )(ent, edge_ends, relation_ids[None], neg_ids, edge_count[None], rel)
    if n_bucket != 2:
        rel_grad = 0.5 * lax.psum(rel_grad, "bucket")
    step = max(128, rows // 2)
    wide = pl.BlockSpec((width, step), lambda i: (0, i))
    line = pl.BlockSpec((1, step), lambda i: (0, i))
    rel_all = pl.BlockSpec((width, nrel), lambda i: (0, 0))
    new_ent, new_state, new_rel = pl.pallas_call(
        update,
        grid=(rows // step,),
        out_shape=(
            jax.ShapeDtypeStruct((width, rows), f32),
            jax.ShapeDtypeStruct((1, rows), f32),
            jax.ShapeDtypeStruct((width, nrel), f32),
        ),
        in_specs=[wide, line, wide, rel_all, pl.BlockSpec((1, nrel), lambda i: (0, 0)), rel_all],
        out_specs=(wide, line, rel_all),
        compiler_params=pltpu.CompilerParams(**params),
    )(ent, entity_state[None], grad, rel, relation_state[None], rel_grad)
    return (new_ent.T, new_state[0], new_rel.T)


def solution(mesh):
    return jax.shard_map(
        local,
        mesh=mesh,
        in_specs=(
            P(("dom", "bucket"), None),
            P(("dom", "bucket")),
            P(),
            P(),
            P(None, ("dom", "bucket")),
            P(("dom", "bucket")),
            P(("dom", "bucket"), "depth"),
            P(("dom", "bucket")),
        ),
        out_specs=(P(("dom", "bucket"), None), P(("dom", "bucket")), P()),
        check_vma=False,
    )
```

```python
import functools

import jax
import jax.numpy as jnp
from jax import lax
from jax.experimental import pallas as pl
from jax.experimental.pallas import tpu as pltpu
from jax.sharding import PartitionSpec as P

entity_rate = 0.1
relation_rate = 1.0
MESH = pl.DeviceIdType.MESH
STRIP = 64
f32, bf16 = jnp.float32, jnp.bfloat16


def dot(a, b):
    return jnp.dot(a, b, preferred_element_type=f32)


def dot_nt(a, b):
    return lax.dot_general(a, b, (((1,), (1,)), ((), ())), preferred_element_type=f32)


def parts_of(value, terms):
    out = []
    for _ in range(terms):
        out.append(value.astype(bf16))
        value = value - out[-1].astype(f32)
    return out


def kernel(
    n_dom,
    block,
    neg_half,
    chunks,
    ent,
    ends_in,
    rel_ids_in,
    neg_in,
    count_in,
    rel,
    grad_out,
    rel_out,
    ent_v,
    info_in,
    left_tab,
    far_tab,
    stage,
    info,
    left_hot,
    high,
    low,
    scores,
    counts,
    fgb,
    from_mate,
    both,
    from_y,
    fin_send,
    fin,
    rg,
    rs0,
    r1,
    rs1,
    r2,
    rs2,
    r3,
    rs3,
    tot,
    ssem,
    rsem,
    lsem,
):
    width, rows = ent.shape
    nrel = rel.shape[1]
    half_rows = rows // 2
    chunk = half_rows // chunks
    d, b, y = lax.axis_index("dom"), lax.axis_index("bucket"), lax.axis_index("depth")
    half = n_dom // 2
    d2 = lax.rem(d + half, n_dom)
    odd = lax.rem(b, 2)
    b2 = b + 1 - 2 * odd
    y2 = 1 - y
    home = odd == d // half
    away = odd != d // half
    partner, mate, ypeer = (d2, b, y), (d, b2, y), (d, b, y2)
    diag, diag2 = (d2, b2, y), (d2, b2, y2)
    used = [0]

    def lanes(side, j=None):
        if j is None:
            return pl.ds(pl.multiple_of(side * half_rows, half_rows), half_rows)
        return pl.ds(pl.multiple_of(side * half_rows + j * chunk, chunk), chunk)

    def spot(side, j):
        return side * chunks + j

    def group(side):
        return pl.ds(side * chunks, chunks)

    def whole(table):
        return jnp.concatenate([table[j] for j in range(2 * chunks)], axis=1)

    def cut(value, j):
        return value[:, j * chunk : (j + 1) * chunk]

    def slots(count):
        used[0] += count
        return used[0] - count

    def copy(k, src, dst, device):
        return pltpu.make_async_remote_copy(
            src_ref=src,
            dst_ref=dst,
            send_sem=ssem.at[k],
            recv_sem=rsem.at[k],
            device_id=device,
            device_id_type=MESH,
        )

    def move(k, src, dst, side, device):
        return [
            copy(k + j, src.at[spot(side, j)], dst.at[spot(side, j)], device)
            for j in range(chunks)
        ]

    load_mine = pltpu.make_async_copy(ent.at[:, lanes(y)], ent_v.at[:, lanes(y)], lsem.at[0])
    load_other = pltpu.make_async_copy(ent.at[:, lanes(y2)], ent_v.at[:, lanes(y2)], lsem.at[1])
    load_mine.start()

    @pl.when(home)
    def _():
        load_other.start()

    info_in[0:2] = ends_in[...]
    info_in[2:3] = rel_ids_in[...]
    info_in[3:4] = jnp.broadcast_to(count_in[...], (1, info_in.shape[1]))
    for c in range(neg_in.shape[0]):
        info_in[4:5, c * neg_half : (c + 1) * neg_half] = neg_in[c : c + 1]
    info_in[5:] = jnp.zeros((info_in.shape[0] - 5, info_in.shape[1]), jnp.int32)

    x2 = d + 1 - 2 * lax.rem(d, 2)
    n_ring = n_dom // 2
    ring = [lax.rem(d + k, n_dom) for k in range(n_dom)]
    barrier = pltpu.get_barrier_semaphore()
    load_mine.wait()
    greeted = [mate, ypeer, diag, diag2] + [(ring[k], b, y) for k in range(1, n_dom)]
    for device in greeted:
        pl.semaphore_signal(barrier, inc=1, device_id=device, device_id_type=MESH)
    pl.semaphore_wait(barrier, len(greeted))

    c_info_home = copy(slots(1), info_in, info.at[1], ypeer)
    c_info_away2 = copy(used[0] - 1, info_in, info.at[1], diag2)
    c_info_away = copy(slots(1), info_in, info.at[0], diag)
    c_left = copy(slots(1), left_tab, far_tab, mate)
    c_stage = move(slots(chunks), stage, far_tab, y, partner)
    k_cross = slots(chunks)
    c_cross = move(k_cross, far_tab, far_tab, y, ypeer)
    c_cross_in = move(k_cross, far_tab, far_tab, y2, ypeer)
    c_mate0 = move(slots(chunks), far_tab, left_tab, y, mate)
    c_mate1 = move(slots(chunks), far_tab, left_tab, y2, mate)

    @pl.when(away)
    def _():
        for j in range(chunks):
            stage[spot(y, j)] = ent_v[:, lanes(y, j)].astype(bf16)
            c_stage[j].start()
        c_info_away.start()
        c_info_away2.start()
        c_info_away.wait()
        c_info_away2.wait()

    @pl.when(home)
    def _():
        load_other.wait()
        for j in range(2 * chunks):
            left_tab[j] = cut(ent_v, j).astype(bf16)
        c_left.start()
        c_info_home.start()
        info[0] = info_in[...]
        c_info_home.wait()

    rel_at = lax.broadcasted_iota(jnp.int32, (nrel, 1), 0)
    neg_lanes = pl.ds(pl.multiple_of(y * neg_half, neg_half), neg_half)
    edge_lanes = pl.ds(pl.multiple_of(y * block, block), block)
    left_ids = info[0, 0:1, edge_lanes]
    right_ids = info[0, 1:2, edge_lanes]
    rel_ids = info[0, 2:3, edge_lanes]
    live = info[0, 3:4, edge_lanes]
    slot_at = y * block + lax.broadcasted_iota(jnp.int32, (1, block), 1)
    active = (slot_at < live).astype(f32)
    negs = jnp.concatenate([info[slot, 4:5, neg_lanes] for slot in range(2)], axis=1)

    def strip(i):
        at = pl.ds(pl.multiple_of(i * STRIP, STRIP), STRIP)
        return at, i * STRIP + lax.broadcasted_iota(jnp.int32, (STRIP, 1), 0)

    def fold(value, join):
        return join(value.reshape(STRIP // 8, 8, block), axis=0)

    def spread(at):
        return jnp.concatenate([counts[at, :]] * (block // 128), axis=1)

    def find(i, carry):
        at, row_at = strip(i)
        hits = jnp.zeros((STRIP, 128), f32)
        for t in range(2 * neg_half // 128):
            hits += (row_at == negs[:, t * 128 : (t + 1) * 128]).astype(f32)
        counts[at, :] = jnp.broadcast_to(jnp.sum(hits, axis=1, keepdims=True), (STRIP, 128))
        left_hot[at, :] = (row_at == left_ids).astype(bf16)
        return carry

    lax.fori_loop(0, rows // STRIP, find, 0)
    rel_hot = (rel_at == rel_ids).astype(bf16)
    scales = dot(jnp.concatenate(parts_of(rel[...], 3), axis=0), rel_hot)
    scaling = scales[:width] + scales[width : 2 * width] + scales[2 * width :]

    @pl.when(home)
    def _():
        for j in range(chunks):
            c_stage[j].wait_recv()
            c_cross[j].start()
            c_mate0[j].start()
        for j in range(chunks):
            c_cross_in[j].wait_recv()
            c_mate1[j].start()

    @pl.when(away)
    def _():
        c_left.wait_recv()
        for j in range(chunks):
            c_mate0[j].wait_recv()
        for j in range(chunks):
            c_mate1[j].wait_recv()

    left_rows = dot(whole(left_tab), left_hot[...])
    queries = (left_rows * scaling).astype(bf16)
    far = whole(far_tab)
    scores[...] = dot(far.T, queries)

    def largest(i, carry):
        at, row_at = strip(i)
        score = scores[at, :]
        best = fold(jnp.where(spread(at) > 0.0, score, -1e30), jnp.max)
        return (
            jnp.maximum(carry[0], best),
            carry[1] + fold(jnp.where(row_at == right_ids, score, 0.0), jnp.sum),
        )

    start = (jnp.full((8, block), -1e30, f32), jnp.zeros((8, block), f32))
    best, hit = lax.fori_loop(0, rows // STRIP, largest, start)
    positive = jnp.sum(hit, axis=0, keepdims=True)
    peak = jnp.maximum(positive, jnp.max(best, axis=0, keepdims=True))

    def exponentials(i, carry):
        at, _ = strip(i)
        count = spread(at)
        shifted = jnp.exp(jnp.where(count > 0.0, scores[at, :], -1e30) - peak)
        scores[at, :] = shifted
        return carry + fold(count * shifted, jnp.sum)

    total = lax.fori_loop(0, rows // STRIP, exponentials, jnp.zeros((8, block), f32))
    pos_exp = jnp.exp(positive - peak)
    denom = pos_exp + jnp.sum(total, axis=0, keepdims=True)
    scale = active / denom
    pos_coef = active * (pos_exp / denom - 1.0)

    def coefficients(i, carry):
        at, row_at = strip(i)
        weights = (scores[at, :] * scale).astype(bf16).astype(f32)
        value = spread(at) * weights + jnp.where(row_at == right_ids, pos_coef, 0.0)
        high[at, :], low[at, :] = parts_of(value, 2)
        return carry

    lax.fori_loop(0, rows // STRIP, coefficients, 0)

    k_far = slots(2)
    c_far = []
    for i, s in enumerate((y2, y)):
        c_far.append(copy(k_far + i, fgb.at[group(s)], from_mate.at[group(s)], mate))
        far_part = dot_nt(queries, high[lanes(s), :]) + dot_nt(queries, low[lanes(s), :])
        for j in range(chunks):
            fgb[spot(s, j)] = cut(far_part, j).astype(bf16)
        c_far[i].start()

    query_grad = dot(far, high[...]) + dot(far, low[...])
    own_terms = (query_grad * scaling).astype(bf16)

    k_away = slots(chunks)
    c_away = move(k_away, both, from_y, y2, ypeer)
    c_away_in = move(k_away, both, from_y, y, ypeer)
    k_home = slots(2)
    c_home, c_home_in = [], []
    for i, (s, o) in enumerate(((y2, y), (y, y2))):
        c_home.append(copy(k_home + i, both.at[group(s)], from_y.at[group(s)], ypeer))
        c_home_in.append(copy(k_home + i, both.at[group(o)], from_y.at[group(o)], ypeer))
    c_fin = move(slots(chunks), fin_send, fin, y, diag)
    k_fin_y = slots(chunks)
    c_fin_y = move(k_fin_y, fin, fin, y, ypeer)
    c_fin_y_in = move(k_fin_y, fin, fin, y2, ypeer)

    def own_half(i, s):
        own_part = dot_nt(own_terms, left_hot[lanes(s), :])
        c_far[i].wait_recv()
        for j in range(chunks):
            at = spot(s, j)
            both[at] = (cut(own_part, j) + from_mate[at].astype(f32)).astype(bf16)

        @pl.when(home)
        def _():
            c_home[i].start()

    own_half(0, y2)

    @pl.when(away)
    def _():
        for c in c_away:
            c.start()

    rel_part = dot_nt(jnp.concatenate(parts_of(query_grad * left_rows, 2), axis=0), rel_hot)
    rel_part = rel_part[:width] + rel_part[width:]
    deep = rg.shape[1]
    for side in range(2):
        rg[side, :width] = rel_part[:, side * (nrel // 2) : (side + 1) * (nrel // 2)]
        rg[side, width:] = jnp.zeros((deep - width, nrel // 2), f32)
    odd2 = 1 - odd
    c_r0 = copy(slots(1), rg.at[odd2], rs0, mate)
    c_r0.start()

    own_half(1, y)

    half_deep = deep // 2
    part = half_deep // n_ring
    x, xpeer, lap = lax.rem(d, 2), (x2, b, y), d // 2

    def half_piece(side):
        return pl.ds(pl.multiple_of(side * half_deep, half_deep), half_deep)

    def piece(side, at):
        return pl.ds(pl.multiple_of(side * half_deep + at * part, part), part)

    laps = [lax.rem(lap + k, n_ring) for k in range(n_ring)]
    peers = [(2 * at + x, b, y) for at in laps]

    def pass_on(j):
        @pl.when(away)
        def _():
            at = spot(y, j)
            c_away_in[j].wait_recv()
            fin_send[at] = (both[at].astype(f32) + from_y[at].astype(f32)).astype(bf16)
            c_fin[j].start()

    def hand_over(j):
        @pl.when(away)
        def _():
            c_fin[j].wait_recv()
            c_fin_y[j].start()
            grad_out[:, lanes(y, j)] = fin[spot(y, j)]

    def take(i, side):
        @pl.when(home)
        def _():
            c_home_in[i].wait_recv()
            for j in range(chunks):
                at = spot(side, j)
                sums = both[at].astype(f32) + from_y[at].astype(f32)
                grad_out[:, lanes(side, j)] = sums.astype(bf16)

    steps = [[] for _ in range(5)]
    for j in range(chunks):
        steps[min(j, 4)].append(j)

    c_r0.wait_recv()
    r1[...] = rg[odd] + rs0[...]
    c_r1 = copy(slots(1), r1.at[half_piece(1 - x)], rs1, xpeer)
    c_r1.start()
    for j in steps[0]:
        pass_on(j)
    c_r1.wait_recv()
    r2[...] = r1[half_piece(x), :] + rs1[...]
    k_r2 = slots(n_ring)
    c_r2 = [
        copy(k_r2 + k, r2.at[piece(0, laps[k])], rs2.at[k], peers[k]) for k in range(1, n_ring)
    ]
    for c in c_r2:
        c.start()
    for j in steps[1]:
        pass_on(j)
    for c in c_r2:
        c.wait_recv()
    r3[...] = r2[piece(0, lap), :] + jnp.sum(rs2[1:], axis=0)
    c_r3 = copy(slots(1), r3, rs3, ypeer)
    c_r3.start()
    for j in steps[2]:
        pass_on(j)
    c_r3.wait_recv()
    tot[odd, piece(x, lap), :] = r3[...] + rs3[...]
    k_t2 = slots(n_ring)
    here = tot.at[odd, piece(x, lap)]
    c_t2, c_t2_in = [], []
    for k in range(1, n_ring):
        there = tot.at[odd, piece(x, laps[n_ring - k])]
        c_t2.append(copy(k_t2 + k, here, here, peers[k]))
        c_t2_in.append(copy(k_t2 + k, there, there, peers[k]))
        c_t2[-1].start()
    for j in steps[3]:
        pass_on(j)
    for c in c_t2_in:
        c.wait_recv()
    mine_t, other_t = tot.at[odd, half_piece(x)], tot.at[odd, half_piece(1 - x)]
    k_t1 = slots(1)
    c_t1 = copy(k_t1, mine_t, mine_t, xpeer)
    c_t1_in = copy(k_t1, other_t, other_t, xpeer)
    c_t1.start()
    for j in steps[4]:
        pass_on(j)
    take(0, y)
    for j in range(chunks // 2):
        hand_over(j)
    c_t1_in.wait_recv()
    k_t0 = slots(1)
    c_t0 = copy(k_t0, tot.at[odd], tot.at[odd], mate)
    c_t0_in = copy(k_t0, tot.at[odd2], tot.at[odd2], mate)
    c_t0.start()
    for j in range(chunks // 2, chunks):
        hand_over(j)
    take(1, y2)

    @pl.when(away)
    def _():
        for j in range(chunks):
            c_fin_y_in[j].wait_recv()
            grad_out[:, lanes(y2, j)] = fin[spot(y2, j)]

    c_t0_in.wait_recv()
    for side in range(2):
        rel_out[:, side * (nrel // 2) : (side + 1) * (nrel // 2)] = tot[side, :width]

    @pl.when(home)
    def _():
        for c in [c_left] + c_cross + c_mate0 + c_mate1 + c_home:
            c.wait_send()

    @pl.when(away)
    def _():
        for c in c_stage + c_away + c_fin + c_fin_y:
            c.wait_send()

    for c in [c_r0, c_r1, c_r3, c_t1, c_t0] + c_far + c_r2 + c_t2:
        c.wait_send()


def adagrad(rate, values, state, grad, values_out, state_out):
    updated = state[...] + jnp.sum(grad * grad, axis=0, keepdims=True) * (1.0 / grad.shape[0])
    values_out[...] = values[...] - grad * (rate / jnp.sqrt(updated))
    if state_out is not None:
        state_out[...] = updated


def update(ent, state, grad, rel, rel_state, rel_grad, ent_out, state_out, rel_out):
    adagrad(entity_rate, ent, state, grad[...].astype(f32), ent_out, state_out)

    @pl.when(pl.program_id(0) == 0)
    def _():
        adagrad(relation_rate, rel, rel_state, rel_grad[...], rel_out, None)


def local(
    entities, entity_state, relations, relation_state, edge_ends, relation_ids, neg_ids, edge_count
):
    rows, width = entities.shape
    nrel = relations.shape[0]
    slots = edge_ends.shape[1]
    blocks, neg_half = neg_ids.shape
    n_dom, n_bucket, n_depth = (lax.axis_size(a) for a in ("dom", "bucket", "depth"))
    assert blocks == n_depth == 2 and n_dom % 2 == 0 and n_bucket % 2 == 0
    assert blocks * neg_half == slots
    chunks = max(1, rows // 2 // 128)
    grain = 8 * n_dom
    deep = -(-width // grain) * grain
    half_rel = nrel // 2
    vmem = pl.BlockSpec(memory_space=pltpu.VMEM)
    table = pltpu.VMEM((2 * chunks, width, rows // (2 * chunks)), bf16)
    spots = pltpu.VMEM((rows, slots // blocks), bf16)
    n_sems = 16 + 7 * chunks + n_dom
    params = dict(vmem_limit_bytes=56 * 1024 * 1024)
    ent, rel = entities.T, relations.T
    grad, rel_grad = pl.pallas_call(
        functools.partial(kernel, n_dom, slots // blocks, neg_half, chunks),
        out_shape=(
            jax.ShapeDtypeStruct((width, rows), bf16),
            jax.ShapeDtypeStruct((width, nrel), f32),
        ),
        in_specs=[pl.BlockSpec(memory_space=pl.ANY)] + [vmem] * 5,
        out_specs=(vmem,) * 2,
        scratch_shapes=[
            pltpu.VMEM((width, rows), f32),
            pltpu.VMEM((8, slots), jnp.int32),
            table,
            table,
            table,
            pltpu.VMEM((2, 8, slots), jnp.int32),
            spots,
            spots,
            spots,
            pltpu.VMEM((rows, slots // blocks), f32),
            pltpu.VMEM((rows, 128), f32),
            table,
            table,
            table,
            table,
            table,
            table,
            pltpu.VMEM((2, deep, half_rel), f32),
            pltpu.VMEM((deep, half_rel), f32),
            pltpu.VMEM((deep, half_rel), f32),
            pltpu.VMEM((deep // 2, half_rel), f32),
            pltpu.VMEM((deep // 2, half_rel), f32),
            pltpu.VMEM((n_dom // 2, deep // n_dom, half_rel), f32),
            pltpu.VMEM((deep // n_dom, half_rel), f32),
            pltpu.VMEM((deep // n_dom, half_rel), f32),
            pltpu.VMEM((2, deep, half_rel), f32),
            pltpu.SemaphoreType.DMA((n_sems,)),
            pltpu.SemaphoreType.DMA((n_sems,)),
            pltpu.SemaphoreType.DMA((2,)),
        ],
        compiler_params=pltpu.CompilerParams(collective_id=0, has_side_effects=True, **params),
    )(ent, edge_ends, relation_ids[None], neg_ids, edge_count[None], rel)
    if n_bucket != 2:
        rel_grad = 0.5 * lax.psum(rel_grad, "bucket")
    step = max(128, rows // 2)
    wide = pl.BlockSpec((width, step), lambda i: (0, i))
    line = pl.BlockSpec((1, step), lambda i: (0, i))
    rel_all = pl.BlockSpec((width, nrel), lambda i: (0, 0))
    new_ent, new_state, new_rel = pl.pallas_call(
        update,
        grid=(rows // step,),
        out_shape=(
            jax.ShapeDtypeStruct((width, rows), f32),
            jax.ShapeDtypeStruct((1, rows), f32),
            jax.ShapeDtypeStruct((width, nrel), f32),
        ),
        in_specs=[wide, line, wide, rel_all, pl.BlockSpec((1, nrel), lambda i: (0, 0)), rel_all],
        out_specs=(wide, line, rel_all),
        compiler_params=pltpu.CompilerParams(**params),
    )(ent, entity_state[None], grad, rel, relation_state[None], rel_grad)
    return (new_ent.T, new_state[0], new_rel.T)


def solution(mesh):
    return jax.shard_map(
        local,
        mesh=mesh,
        in_specs=(
            P(("dom", "bucket"), None),
            P(("dom", "bucket")),
            P(),
            P(),
            P(None, ("dom", "bucket")),
            P(("dom", "bucket")),
            P(("dom", "bucket"), "depth"),
            P(("dom", "bucket")),
        ),
        out_specs=(P(("dom", "bucket"), None), P(("dom", "bucket")), P()),
        check_vma=False,
    )
```

```python
import functools

import jax
import jax.numpy as jnp
from jax import lax
from jax.experimental import pallas as pl
from jax.experimental.pallas import tpu as pltpu
from jax.sharding import PartitionSpec as P

entity_rate = 0.1
relation_rate = 1.0
MESH = pl.DeviceIdType.MESH
STRIP = 32
f32, bf16 = jnp.float32, jnp.bfloat16


def dot(a, b):
    return jnp.dot(a, b, preferred_element_type=f32)


def dot_nt(a, b):
    return lax.dot_general(a, b, (((1,), (1,)), ((), ())), preferred_element_type=f32)


def parts_of(value, terms):
    out = []
    for _ in range(terms):
        out.append(value.astype(bf16))
        value = value - out[-1].astype(f32)
    return out


def kernel(
    n_dom,
    block,
    neg_half,
    chunks,
    ent,
    ends_in,
    rel_ids_in,
    neg_in,
    count_in,
    rel,
    grad_out,
    square_out,
    rel_out,
    ent_v,
    info_in,
    left_tab,
    far_tab,
    stage,
    info,
    left_hot,
    high,
    low,
    scores,
    counts,
    fgb,
    from_mate,
    fin_send,
    fin,
    square_send,
    square,
    rg,
    rs0,
    r1,
    rs1,
    r2,
    rs2,
    tot,
    ssem,
    rsem,
    lsem,
):
    width, rows = ent.shape
    nrel = rel.shape[1]
    slot_count = ends_in.shape[1]
    half_rows = rows // 2
    chunk = half_rows // chunks
    d, b, y = lax.axis_index("dom"), lax.axis_index("bucket"), lax.axis_index("depth")
    half = n_dom // 2
    d2 = lax.rem(d + half, n_dom)
    odd = lax.rem(b, 2)
    b2 = b + 1 - 2 * odd
    y2 = 1 - y
    home = odd == d // half
    away = odd != d // half
    partner, mate, ypeer = (d2, b, y), (d, b2, y), (d, b, y2)
    diag, diag2 = (d2, b2, y), (d2, b2, y2)
    used = [0]

    def lanes(side, j=None):
        if j is None:
            return pl.ds(pl.multiple_of(side * half_rows, half_rows), half_rows)
        return pl.ds(pl.multiple_of(side * half_rows + j * chunk, chunk), chunk)

    def slots(count):
        used[0] += count
        return used[0] - count

    def copy(k, src, dst, device):
        return pltpu.make_async_remote_copy(
            src_ref=src,
            dst_ref=dst,
            send_sem=ssem.at[k],
            recv_sem=rsem.at[k],
            device_id=device,
            device_id_type=MESH,
        )

    def move(k, src, dst, side, device):
        return [
            copy(k + j, src.at[:, lanes(side, j)], dst.at[:, lanes(side, j)], device)
            for j in range(chunks)
        ]

    load_mine = pltpu.make_async_copy(ent.at[:, lanes(y)], ent_v.at[:, lanes(y)], lsem.at[0])
    load_other = pltpu.make_async_copy(ent.at[:, lanes(y2)], ent_v.at[:, lanes(y2)], lsem.at[1])
    load_mine.start()

    @pl.when(home)
    def _():
        load_other.start()

    info_in[0:2] = ends_in[...]
    info_in[2:3] = rel_ids_in[...]
    info_in[3:4] = jnp.broadcast_to(count_in[...], (1, info_in.shape[1]))
    for c in range(neg_in.shape[0]):
        info_in[4:5, c * neg_half : (c + 1) * neg_half] = neg_in[c : c + 1]
    info_in[5:] = jnp.zeros((info_in.shape[0] - 5, info_in.shape[1]), jnp.int32)

    x2 = d + 1 - 2 * lax.rem(d, 2)
    n_ring = n_dom // 2
    ring = [lax.rem(d + k, n_dom) for k in range(n_dom)]
    barrier = pltpu.get_barrier_semaphore()
    load_mine.wait()
    greeted = [mate, ypeer, diag, diag2] + [(ring[k], b, y) for k in range(1, n_dom)]
    for device in greeted:
        pl.semaphore_signal(barrier, inc=1, device_id=device, device_id_type=MESH)
    pl.semaphore_wait(barrier, len(greeted))

    c_info_home = copy(slots(1), info_in, info.at[1], ypeer)
    c_info_away2 = copy(used[0] - 1, info_in, info.at[1], diag2)
    c_info_away = copy(slots(1), info_in, info.at[0], diag)
    c_left = copy(slots(1), left_tab, far_tab, mate)
    c_stage = move(slots(chunks), stage, far_tab, y, partner)
    k_cross = slots(chunks)
    c_cross = move(k_cross, far_tab, far_tab, y, ypeer)
    c_cross_in = move(k_cross, far_tab, far_tab, y2, ypeer)
    c_mate0 = move(slots(chunks), far_tab, left_tab, y, mate)
    c_mate1 = move(slots(chunks), far_tab, left_tab, y2, mate)

    @pl.when(away)
    def _():
        for j in range(chunks):
            stage[:, lanes(y, j)] = ent_v[:, lanes(y, j)].astype(bf16)
            c_stage[j].start()
        c_info_away.start()
        c_info_away2.start()
        c_info_away.wait()
        c_info_away2.wait()

    @pl.when(home)
    def _():
        load_other.wait()
        left_tab[...] = ent_v[...].astype(bf16)
        c_left.start()
        c_info_home.start()
        info[0] = info_in[...]
        c_info_home.wait()

    rel_at = lax.broadcasted_iota(jnp.int32, (nrel, 1), 0)
    left_ids = info[0, 0:1]
    right_ids = info[0, 1:2]
    rel_ids = info[0, 2:3]
    live = info[0, 3:4]
    slot_at = lax.broadcasted_iota(jnp.int32, (1, slot_count), 1)
    active = (slot_at < live).astype(f32)
    blocks = slot_count // block

    def strip(i):
        at = pl.ds(pl.multiple_of(i * STRIP, STRIP), STRIP)
        return at, i * STRIP + lax.broadcasted_iota(jnp.int32, (STRIP, 1), 0)

    def fold(value, join):
        return join(value.reshape(STRIP // 8, 8, slot_count), axis=0)

    def spread(at):
        return jnp.concatenate([counts[c, at, :] for c in range(blocks) for _ in range(block // 128)], axis=1)

    def find(i, carry):
        at, row_at = strip(i)
        for c in range(blocks):
            hits = jnp.zeros((STRIP, 128), f32)
            for slot in range(2):
                for t in range(c * neg_half, (c + 1) * neg_half, 128):
                    hits += (row_at == info[slot, 4:5, t : t + 128]).astype(f32)
            found = jnp.sum(hits, axis=1, keepdims=True)
            counts[c, at, :] = jnp.broadcast_to(found, (STRIP, 128))
        left_hot[at, :] = (row_at == left_ids).astype(bf16)
        return carry

    lax.fori_loop(0, rows // STRIP, find, 0)
    rel_hot = (rel_at == rel_ids).astype(bf16)
    scales = dot(jnp.concatenate(parts_of(rel[...], 3), axis=0), rel_hot)
    scaling = scales[:width] + scales[width : 2 * width] + scales[2 * width :]

    @pl.when(home)
    def _():
        for j in range(chunks):
            c_stage[j].wait_recv()
            c_cross[j].start()
            c_mate0[j].start()
        for j in range(chunks):
            c_cross_in[j].wait_recv()
            c_mate1[j].start()

    @pl.when(away)
    def _():
        c_left.wait_recv()
        for j in range(chunks):
            c_mate0[j].wait_recv()
        for j in range(chunks):
            c_mate1[j].wait_recv()

    left_rows = dot(left_tab[...], left_hot[...])
    queries = (left_rows * scaling).astype(bf16)
    far = far_tab[...]
    scores[...] = dot(far.T, queries)

    def largest(i, carry):
        at, row_at = strip(i)
        score = scores[at, :]
        best = fold(jnp.where(spread(at) > 0.0, score, -1e30), jnp.max)
        return (
            jnp.maximum(carry[0], best),
            carry[1] + fold(jnp.where(row_at == right_ids, score, 0.0), jnp.sum),
        )

    start = (jnp.full((8, slot_count), -1e30, f32), jnp.zeros((8, slot_count), f32))
    best, hit = lax.fori_loop(0, rows // STRIP, largest, start)
    positive = jnp.sum(hit, axis=0, keepdims=True)
    peak = jnp.maximum(positive, jnp.max(best, axis=0, keepdims=True))

    def exponentials(i, carry):
        at, _ = strip(i)
        count = spread(at)
        shifted = jnp.exp(jnp.where(count > 0.0, scores[at, :], -1e30) - peak)
        scores[at, :] = shifted
        return carry + fold(count * shifted, jnp.sum)

    total = lax.fori_loop(0, rows // STRIP, exponentials, jnp.zeros((8, slot_count), f32))
    pos_exp = jnp.exp(positive - peak)
    denom = pos_exp + jnp.sum(total, axis=0, keepdims=True)
    scale = active / denom
    pos_coef = active * (pos_exp / denom - 1.0)

    def coefficients(i, carry):
        at, row_at = strip(i)
        weights = (scores[at, :] * scale).astype(bf16).astype(f32)
        value = spread(at) * weights + jnp.where(row_at == right_ids, pos_coef, 0.0)
        high[at, :], low[at, :] = parts_of(value, 2)
        return carry

    lax.fori_loop(0, rows // STRIP, coefficients, 0)

    far_part = dot_nt(queries, high[lanes(y), :]) + dot_nt(queries, low[lanes(y), :])
    c_far = move(slots(chunks), fgb, from_mate, y, mate)
    for j in range(chunks):
        fgb[:, lanes(y, j)] = far_part[:, j * chunk : (j + 1) * chunk]
        c_far[j].start()

    query_grad = dot(far, high[...]) + dot(far, low[...])
    own_part = dot_nt((query_grad * scaling).astype(bf16), left_hot[lanes(y), :])

    c_fin = move(slots(chunks), fin_send, fin, y, diag)
    k_fin_y = slots(chunks)
    c_fin_y = move(k_fin_y, fin, fin, y, ypeer)
    c_fin_y_in = move(k_fin_y, fin, fin, y2, ypeer)
    for j in range(chunks):
        at = lanes(y, j)
        c_far[j].wait_recv()
        sums = own_part[:, j * chunk : (j + 1) * chunk] + from_mate[:, at]

        squares = jnp.broadcast_to(jnp.sum(sums * sums, axis=0, keepdims=True), (8, chunk))

        @pl.when(home)
        def _():
            square[:, at] = squares
            fin[:, at] = sums.astype(bf16)
            c_fin_y[j].start()

        @pl.when(away)
        def _():
            square_send[:, at] = squares
            fin_send[:, at] = sums.astype(bf16)
            c_fin[j].start()

    mine, other = square.at[:, lanes(y)], square.at[:, lanes(y2)]
    c_square = copy(slots(1), square_send.at[:, lanes(y)], mine, diag)
    k_square = slots(1)
    c_square_y = copy(k_square, mine, mine, ypeer)
    c_square_in = copy(k_square, other, other, ypeer)

    @pl.when(home)
    def _():
        c_square_y.start()

    @pl.when(away)
    def _():
        c_square.start()

    rel_part = dot_nt(jnp.concatenate(parts_of(query_grad * left_rows, 2), axis=0), rel_hot)
    rel_part = rel_part[:width] + rel_part[width:]
    deep = rg.shape[1]
    for side in range(2):
        rg[side, :width] = rel_part[:, side * (nrel // 2) : (side + 1) * (nrel // 2)]
        rg[side, width:] = jnp.zeros((deep - width, nrel // 2), f32)
    odd2 = 1 - odd
    c_r0 = copy(slots(1), rg.at[odd2], rs0, mate)
    c_r0.start()

    half_deep = deep // 2
    part = half_deep // n_ring
    x, xpeer, lap = lax.rem(d, 2), (x2, b, y), d // 2

    def half_piece(side):
        return pl.ds(pl.multiple_of(side * half_deep, half_deep), half_deep)

    def piece(side, at):
        return pl.ds(pl.multiple_of(side * half_deep + at * part, part), part)

    laps = [lax.rem(lap + k, n_ring) for k in range(n_ring)]
    peers = [(2 * at + x, b, y) for at in laps]

    c_r0.wait_recv()
    r1[...] = rg[odd] + rs0[...]
    c_r1 = copy(slots(1), r1.at[half_piece(1 - x)], rs1, xpeer)
    c_r1.start()
    c_r1.wait_recv()
    r2[...] = r1[half_piece(x), :] + rs1[...]
    k_r2 = slots(n_ring)
    c_r2 = [
        copy(k_r2 + k, r2.at[piece(0, laps[k])], rs2.at[k], peers[k]) for k in range(1, n_ring)
    ]
    for c in c_r2:
        c.start()

    for c in c_r2:
        c.wait_recv()
    tot[odd, piece(x, lap), :] = r2[piece(0, lap), :] + jnp.sum(rs2[1:], axis=0)
    k_t2 = slots(n_ring)
    here = tot.at[odd, piece(x, lap)]
    c_t2, c_t2_in = [], []
    for k in range(1, n_ring):
        there = tot.at[odd, piece(x, laps[n_ring - k])]
        c_t2.append(copy(k_t2 + k, here, here, peers[k]))
        c_t2_in.append(copy(k_t2 + k, there, there, peers[k]))
        c_t2[-1].start()

    for c in c_t2_in:
        c.wait_recv()
    mine_t, other_t = tot.at[odd, half_piece(x)], tot.at[odd, half_piece(1 - x)]
    k_t1 = slots(1)
    c_t1 = copy(k_t1, mine_t, mine_t, xpeer)
    c_t1_in = copy(k_t1, other_t, other_t, xpeer)
    c_t1.start()

    @pl.when(away)
    def _():
        c_square.wait_recv()
        c_square_y.start()
        for j in range(chunks):
            c_fin[j].wait_recv()
            c_fin_y[j].start()

    c_t1_in.wait_recv()
    k_t0 = slots(1)
    c_t0 = copy(k_t0, tot.at[odd], tot.at[odd], mate)
    c_t0_in = copy(k_t0, tot.at[odd2], tot.at[odd2], mate)
    c_t0.start()

    grad_out[:, lanes(y)] = fin[:, lanes(y)]
    for j in range(chunks):
        c_fin_y_in[j].wait_recv()
        grad_out[:, lanes(y2, j)] = fin[:, lanes(y2, j)]

    c_square_in.wait_recv()
    square_out[...] = square[0:1]
    c_t0_in.wait_recv()
    for side in range(2):
        rel_out[:, side * (nrel // 2) : (side + 1) * (nrel // 2)] = tot[side, :width]

    @pl.when(home)
    def _():
        for c in [c_left] + c_cross + c_mate0 + c_mate1:
            c.wait_send()

    @pl.when(away)
    def _():
        for c in c_stage + c_fin + [c_square]:
            c.wait_send()

    for c in [c_r0, c_r1, c_t1, c_t0, c_square_y] + c_far + c_fin_y + c_r2 + c_t2:
        c.wait_send()


def adagrad(rate, values, state, grad, squares, values_out, state_out):
    updated = state[...] + squares * (1.0 / grad.shape[0])
    values_out[...] = values[...] - grad * (rate / jnp.sqrt(updated))
    if state_out is not None:
        state_out[...] = updated


def update(ent, state, grad, squares, rel, rel_state, rel_grad, ent_out, state_out, rel_out):
    adagrad(entity_rate, ent, state, grad[...].astype(f32), squares[...], ent_out, state_out)

    @pl.when(pl.program_id(0) == 0)
    def _():
        total = rel_grad[...]
        rel_squares = jnp.sum(total * total, axis=0, keepdims=True)
        adagrad(relation_rate, rel, rel_state, total, rel_squares, rel_out, None)


def local(
    entities, entity_state, relations, relation_state, edge_ends, relation_ids, neg_ids, edge_count
):
    rows, width = entities.shape
    nrel = relations.shape[0]
    slots = edge_ends.shape[1]
    blocks, neg_half = neg_ids.shape
    n_dom, n_bucket, n_depth = (lax.axis_size(a) for a in ("dom", "bucket", "depth"))
    assert blocks == n_depth == 2 and n_dom % 2 == 0 and n_bucket % 2 == 0
    assert blocks * neg_half == slots
    chunks = max(1, rows // 2 // 128)
    grain = 8 * n_dom
    deep = -(-width // grain) * grain
    half_rel = nrel // 2
    vmem = pl.BlockSpec(memory_space=pltpu.VMEM)
    table = pltpu.VMEM((width, rows), bf16)
    spots = pltpu.VMEM((rows, slots), bf16)
    n_sems = 16 + 7 * chunks + n_dom
    params = dict(vmem_limit_bytes=56 * 1024 * 1024)
    ent, rel = entities.T, relations.T
    grad, squares, rel_grad = pl.pallas_call(
        functools.partial(kernel, n_dom, slots // blocks, neg_half, chunks),
        out_shape=(
            jax.ShapeDtypeStruct((width, rows), bf16),
            jax.ShapeDtypeStruct((1, rows), f32),
            jax.ShapeDtypeStruct((width, nrel), f32),
        ),
        in_specs=[pl.BlockSpec(memory_space=pl.ANY)] + [vmem] * 5,
        out_specs=(vmem,) * 3,
        scratch_shapes=[
            pltpu.VMEM((width, rows), f32),
            pltpu.VMEM((8, slots), jnp.int32),
            table,
            table,
            table,
            pltpu.VMEM((2, 8, slots), jnp.int32),
            spots,
            spots,
            spots,
            pltpu.VMEM((rows, slots), f32),
            pltpu.VMEM((blocks, rows, 128), f32),
            pltpu.VMEM((width, rows), f32),
            pltpu.VMEM((width, rows), f32),
            table,
            table,
            pltpu.VMEM((8, rows), f32),
            pltpu.VMEM((8, rows), f32),
            pltpu.VMEM((2, deep, half_rel), f32),
            pltpu.VMEM((deep, half_rel), f32),
            pltpu.VMEM((deep, half_rel), f32),
            pltpu.VMEM((deep // 2, half_rel), f32),
            pltpu.VMEM((deep // 2, half_rel), f32),
            pltpu.VMEM((n_dom // 2, deep // n_dom, half_rel), f32),
            pltpu.VMEM((2, deep, half_rel), f32),
            pltpu.SemaphoreType.DMA((n_sems,)),
            pltpu.SemaphoreType.DMA((n_sems,)),
            pltpu.SemaphoreType.DMA((2,)),
        ],
        compiler_params=pltpu.CompilerParams(collective_id=0, has_side_effects=True, **params),
    )(ent, edge_ends, relation_ids[None], neg_ids, edge_count[None], rel)
    if n_bucket != 2:
        rel_grad = 0.5 * lax.psum(rel_grad, "bucket")
    step = max(128, rows // 2)
    wide = pl.BlockSpec((width, step), lambda i: (0, i))
    line = pl.BlockSpec((1, step), lambda i: (0, i))
    rel_all = pl.BlockSpec((width, nrel), lambda i: (0, 0))
    new_ent, new_state, new_rel = pl.pallas_call(
        update,
        grid=(rows // step,),
        out_shape=(
            jax.ShapeDtypeStruct((width, rows), f32),
            jax.ShapeDtypeStruct((1, rows), f32),
            jax.ShapeDtypeStruct((width, nrel), f32),
        ),
        in_specs=[wide, line, wide, line, rel_all, pl.BlockSpec((1, nrel), lambda i: (0, 0)), rel_all],
        out_specs=(wide, line, rel_all),
        compiler_params=pltpu.CompilerParams(**params),
    )(ent, entity_state[None], grad, squares, rel, relation_state[None], rel_grad)
    return (new_ent.T, new_state[0], new_rel.T)


def solution(mesh):
    return jax.shard_map(
        local,
        mesh=mesh,
        in_specs=(
            P(("dom", "bucket"), None),
            P(("dom", "bucket")),
            P(),
            P(),
            P(None, ("dom", "bucket")),
            P(("dom", "bucket")),
            P(("dom", "bucket"), "depth"),
            P(("dom", "bucket")),
        ),
        out_specs=(P(("dom", "bucket"), None), P(("dom", "bucket")), P()),
        check_vma=False,
    )
```
